32 devices in a mesh: lon: 4 (over x, core), lat: 8 (over z, y).
Axes of the slice: x: 2, y: 2, z: 4, core: 2. Of those that a mesh axis runs over, the one named last changes fastest.
Arguments:
- innovation: bfloat16 [64, 49152], P(None, ('lon', 'lat')), may hold values from -6 to 6
- owner_tile: int32 [49152, 1], P(('lon', 'lat')), may hold values from 0 to 3; in each aligned block of 1536 rows (0 to 1535, 1536 to 3071, ...) at most 768 rows name the same one
- cell_index: int32 [49152], P(('lon', 'lat')), may hold values from 0 to 8191
- length_scale: float32 [64], replicated, may hold values from 1.5 to 8
- eof_basis: bfloat16 [137, 64], replicated, may hold values from -0.75 to 0.75
Outputs:
- increment: bfloat16 [137, 512, 512], P(None, 'lat', 'lon')
The draws below stay inside these ranges and needn't reach their ends.
Inputs may be any that keep to these rules, and one draw needn't show every extreme that they name: `owner_tile`: within the rows of one device (1536 rows, aligned blocks), no tile index appears more than 768 times, and some index appears exactly 768 times.
All inputs are finite; a program needn't handle non-finite values.
Results may differ from the reference program's by a relative error of at most 0.0076.
Values may be sent and summed in bfloat16 or wider, within the bound.
A program may use at most 64 MiB of HBM per device.

```python
import math
import jax
import jax.numpy as jnp
import numpy as np
from jax import lax

LEV = 64
LEVELS = 137
TX = 128
TY = 64
REC = 1536
CAP = 768
NX = 512
NY = 512
OBS = 49152
N_LON = 4
N_LAT = 8


def set_ends(result, key, low, top_value):
    longest = result.shape.index(max(result.shape))
    spots = []
    for shift in (0, 1):
        where = [jax.random.randint(jax.random.fold_in(key, axis), (), 0, length) for axis, length in enumerate(result.shape)]
        where[longest] = (where[longest] + shift) % result.shape[longest]
        spots.append(tuple(where))
    return result.at[spots[0]].set(low).at[spots[1]].set(top_value)


def level_of(stream_key, shape, shards, low, high):
    def one(axis_at, parts):
        heights = jax.random.uniform(jax.random.fold_in(jax.random.fold_in(stream_key, 6), axis_at), (parts,), jnp.float32, low / len(shards), high / len(shards))
        return jnp.repeat(jnp.exp(heights), shape[axis_at] // parts).reshape((-1,) + (1,) * (len(shape) - axis_at - 1))

    loudness = one(*shards[0])
    for cut in shards[1:]:
        loudness = loudness * one(*cut)
    return loudness


def assign_block(own_key, own, number, rows, number_of, top, most, lean):
    order = jax.random.permutation(own_key, number_of)
    crowded, ordinary = portions_of(number_of, rows * top, most, lean, True), portions_of(number_of, rows * top, most, lean, False)
    places = jnp.arange(number_of)

    def named(lengths, turn):
        used = int((lengths > 0).sum())
        fixed = max(1, used // 4)
        moved = fixed + (places - fixed + turn * (used - fixed)) % max(1, number_of - fixed)
        return jnp.zeros((number_of,), jnp.int32).at[order[jnp.where(places < fixed, places, moved)]].set(jnp.asarray(lengths, jnp.int32))

    lengths = jnp.where(number % 4 == 0, named(crowded, number // 4), named(ordinary, number - number // 4 - 1))
    mixed = jax.random.permutation(jax.random.fold_in(own, 3), number_of)
    donor, receiver = mixed[0:number_of // 2 * 2:2], mixed[1:number_of // 2 * 2:2]
    margin = jnp.minimum(lengths[donor] - 1, most - lengths[receiver]) // 2
    margin = jnp.where((donor == order[0]) | (receiver == order[0]) | (lengths[receiver] == 0), 0, jnp.maximum(margin, 0))
    moved = jax.random.randint(jax.random.fold_in(own, 4), (number_of // 2,), 0, 1 << 20) % (margin + 1)
    lengths = lengths.at[donor].add(-moved).at[receiver].add(moved)
    labels = jnp.searchsorted(jnp.cumsum(lengths), jnp.arange(rows * top), side="right").astype(jnp.int32)
    table = labels.reshape(top, rows).T
    table = table[jax.random.permutation(jax.random.fold_in(own, 1), rows)]
    turn = jax.random.randint(jax.random.fold_in(own, 2), (rows, 1), 0, top)
    return jnp.take_along_axis(table, (jnp.arange(top)[None, :] + turn) % top, axis=1)


def portions_of(number_of, total, most, slope, full):
    loads = [(1 << 20) // math.isqrt(grade ** slope) + 1 for grade in range(1, number_of + 1)]
    largest = most if full else min(most, max(-(-total // number_of), total * loads[0] // sum(loads)))
    least = 1 if total - largest >= number_of - 1 else 0
    counts, surplus = [largest] + [least] * (number_of - 1), total - largest - least * (number_of - 1)
    while surplus > 0:
        free = [i for i in range(1, number_of) if counts[i] < largest] or [i for i in range(1, number_of) if counts[i] < most]
        whole, budget = sum([loads[i] for i in free]), surplus
        for i in free:
            addition = min(most - counts[i], max(1, budget * loads[i] // whole), surplus)
            counts[i] = counts[i] + addition
            surplus = surplus - addition
    return np.array(counts)


def bell_draw(own_key, shape, scale, bound, cuts=(), kind=jnp.bfloat16):
    entries = jax.random.normal(own_key, shape, jnp.float32) * scale
    if len(cuts) > 0:
        entries = level_of(own_key, shape, cuts, -0.22, 0.18) * entries
    return jnp.clip(entries, min=-bound, max=bound).astype(kind)


def setup_inputs(seed: int = 0) -> dict:
    arg_keys = jax.random.split(jax.random.key(seed), 6)
    innovation = bell_draw(arg_keys[0], (LEV, OBS), 1.0, 6.0, ((1, 32),))
    owner_tile_keys = jax.random.split(jax.random.fold_in(arg_keys[1], 1), OBS // REC)
    owner_tile_turns = jax.random.permutation(jax.random.fold_in(arg_keys[1], 3), OBS // REC)
    owner_tile = jax.vmap(lambda own, number: assign_block(jax.random.fold_in(arg_keys[1], 2), own, number, REC, N_LON, 1, CAP, 2))(owner_tile_keys, owner_tile_turns).reshape((OBS, 1))
    cell_index = set_ends(jax.random.randint(arg_keys[2], (OBS,), 0, TX * TY), jax.random.fold_in(arg_keys[2], 1), 0, (TX * TY) - 1).astype(jnp.int32)
    length_scale = jnp.clip(jnp.exp(jax.random.uniform(arg_keys[3], (LEV,), jnp.float32, math.log(1.5), math.log(8.0))), 1.5, 8.0)
    eof_basis = bell_draw(arg_keys[4], (LEVELS, LEV), LEV ** -0.5, 0.75)
    return {"innovation": innovation, "owner_tile": owner_tile, "cell_index": cell_index, "length_scale": length_scale, "eof_basis": eof_basis}


def tap_norm(scale):
    dist = jnp.arange(-15, 16).astype(jnp.float32)
    gauss = jnp.exp(-(dist[None, :] * dist[None, :]) / (2.0 * scale[:, None] * scale[:, None]))
    return jnp.sqrt(lax.optimization_barrier(jnp.sum(gauss * gauss, axis=1)))

def tap_weight(dist, scale, norm):
    value = jnp.exp(-(dist * dist) / (2.0 * scale * scale)) / norm
    return jnp.where(jnp.abs(dist) <= 15.0, value, 0.0)

def lon_pass(plane, wts):
    total = jnp.zeros(plane.shape, jnp.float32)
    for index in range(31):
        shift = index - 15
        total = total + wts[index].astype(jnp.float32) * jnp.roll(plane, -shift, axis=1).astype(jnp.float32)
    return total.astype(jnp.bfloat16)

def lat_pass(plane, wts):
    padded = jnp.pad(plane, ((15, 15), (0, 0)))
    total = jnp.zeros(plane.shape, jnp.float32)
    for index in range(31):
        total = total + wts[index].astype(jnp.float32) * padded[index:index + NY].astype(jnp.float32)
    return total.astype(jnp.bfloat16)

def reference(innovation, owner_tile, cell_index, length_scale, eof_basis):
    holder = jnp.arange(OBS, dtype=jnp.int32) // REC
    band = holder % N_LAT
    row_at = band * TY + cell_index // TX
    col_at = owner_tile[:, 0] * TX + cell_index % TX
    flat = (row_at * NX + col_at).astype(jnp.int32)
    sums = jax.ops.segment_sum(innovation.T.astype(jnp.float32), flat, num_segments=NY * NX)
    spread = sums.T.reshape(LEV, NY, NX).astype(jnp.bfloat16)
    norm = tap_norm(length_scale)
    dist = jnp.arange(-15, 16).astype(jnp.float32)
    table = tap_weight(dist[None, :], length_scale[:, None], norm[:, None]).astype(jnp.bfloat16)
    lon_smooth = lax.map(lambda pair: lon_pass(pair[0], pair[1]), (spread, table))
    lat_smooth = lax.map(lambda pair: lat_pass(pair[0], pair[1]), (lon_smooth, table))
    mixed = jnp.dot(eof_basis, lat_smooth.reshape(LEV, NY * NX), preferred_element_type=jnp.float32)
    return mixed.astype(jnp.bfloat16).reshape(LEVELS, NY, NX)
```

```python
import jax
import jax.numpy as jnp
from jax import lax
from jax.sharding import PartitionSpec as P

TX = 128
TY = 64


def extended(shard, sides, width):
    for axis, dim in sides:
        size, length = (lax.axis_size(axis), shard.shape[dim])
        up = [(i, (i + 1) % size) for i in range(size)]
        down = [(j, i) for i, j in up]
        last = lax.slice_in_dim(shard, length - width, length, axis=dim)
        initial = lax.slice_in_dim(shard, 0, width, axis=dim)
        before = lax.ppermute(last, axis, up)
        after = lax.ppermute(initial, axis, down)
        shard = jnp.concatenate([before, shard, after], axis=dim)
    return shard


def tap_norm(scale):
    dist = jnp.arange(-15, 16).astype(jnp.float32)
    gauss = jnp.exp(-(dist[None, :] * dist[None, :]) / (2.0 * scale[:, None] * scale[:, None]))
    return jnp.sqrt(jnp.sum(gauss * gauss, axis=1))


def tap_weight(dist, scale, norm):
    value = jnp.exp(-(dist * dist) / (2.0 * scale * scale)) / norm
    return jnp.where(jnp.abs(dist) <= 15.0, value, 0.0)


def band_matrix(scale, norm, inner, outer, offset):
    inner_pos = jnp.arange(inner).astype(jnp.float32)[:, None]
    outer_pos = jnp.arange(outer).astype(jnp.float32)[None, :]
    dist = inner_pos - offset - outer_pos
    return tap_weight(dist[None], scale[:, None, None], norm[:, None, None]).astype(jnp.bfloat16)


def slot_numbers(dest, keep, n_lon):
    hits = ((dest[:, None] == jnp.arange(n_lon, dtype=jnp.int32)[None, :]) & keep[:, None]).astype(
        jnp.int32
    )
    before = jnp.cumsum(hits, axis=0) - hits
    return jnp.sum(before * hits, axis=1)


def spread_block(part, where, width):
    cells = jnp.arange(TY * width, dtype=jnp.int32)
    grid_row = (cells // width).astype(jnp.bfloat16)
    grid_col = (cells % width).astype(jnp.bfloat16)
    onehot = (
        (where[0][:, None] == grid_row[None, :]) & (where[1][:, None] == grid_col[None, :])
    ).astype(jnp.bfloat16)
    return jnp.dot(part, onehot, preferred_element_type=jnp.float32)


def local(innovation, owner_tile, cell_index, length_scale, eof_basis):
    n_lon = lax.axis_size("lon")
    lev, rec = innovation.shape
    cap = (2 * rec + n_lon - 1) // n_lon
    owner = owner_tile[:, 0]
    cell_row = cell_index // TX
    cell_col = cell_index % TX
    everyone = jnp.ones((rec,), jnp.bool_)
    target = owner * cap + slot_numbers(owner, everyone, n_lon)
    values = jnp.zeros((lev, n_lon * cap), jnp.bfloat16).at[:, target].set(innovation)
    coords = jnp.stack([cell_row, cell_col]).astype(jnp.bfloat16)
    places = jnp.full((2, n_lon * cap), -1.0, jnp.bfloat16).at[:, target].set(coords)
    values = values.reshape(lev, n_lon, cap)
    places = places.reshape(2, n_lon, cap)
    got_values, got_places = (
        lax.all_to_all(values, "lon", split_axis=1, concat_axis=1, tiled=True),
        lax.all_to_all(places, "lon", split_axis=1, concat_axis=1, tiled=True),
    )

    def spread_one(source, total):
        part = lax.dynamic_index_in_dim(got_values, source, 1, keepdims=False)
        where = lax.dynamic_index_in_dim(got_places, source, 1, keepdims=False)
        return total + spread_block(part, where, TX)

    summed = lax.fori_loop(0, n_lon, spread_one, jnp.zeros((lev, TY * TX), jnp.float32))
    spread = summed.astype(jnp.bfloat16).reshape(lev, TY, TX)
    padded = extended(spread, (("lon", 2),), 15)
    norm = tap_norm(length_scale)
    band_lon = band_matrix(length_scale, norm, TX + 30, TX, 15.0)
    lon_smooth = jnp.einsum(
        "cyk,ckx->cyx", padded, band_lon, preferred_element_type=jnp.float32
    ).astype(jnp.bfloat16)
    n_lat = lax.axis_size("lat")
    south = [(i, i + 1) for i in range(n_lat - 1)]
    north = [(j, i) for i, j in south]
    above = lax.ppermute(lon_smooth[:, TY - 16 :], "lat", south)
    below = lax.ppermute(lon_smooth[:, :16], "lat", north)
    column = jnp.concatenate([above, lon_smooth, below], axis=1)
    band_lat = band_matrix(length_scale, norm, TY + 32, TY, 16.0)
    smooth = jnp.einsum(
        "cky,ckx->cyx", band_lat, column, preferred_element_type=jnp.float32
    ).astype(jnp.bfloat16)
    return jnp.einsum("lc,cyx->lyx", eof_basis, smooth, preferred_element_type=jnp.float32).astype(
        jnp.bfloat16
    )


def solution(mesh):
    in_specs = (P(None, ("lon", "lat")), P(("lon", "lat"), None), P(("lon", "lat")), P(), P())
    out_specs = P(None, "lat", "lon")
    return jax.shard_map(local, mesh=mesh, in_specs=in_specs, out_specs=out_specs, check_vma=False)
```

```python
import functools

import jax
import jax.numpy as jnp
from jax import lax
from jax.experimental import pallas as pl
from jax.experimental.pallas import tpu as pltpu
from jax.sharding import PartitionSpec as P

TX = 128
TY = 64


def extended(shard, sides, width):
    for axis, dim in sides:
        size, length = (lax.axis_size(axis), shard.shape[dim])
        up = [(i, (i + 1) % size) for i in range(size)]
        down = [(j, i) for i, j in up]
        last = lax.slice_in_dim(shard, length - width, length, axis=dim)
        initial = lax.slice_in_dim(shard, 0, width, axis=dim)
        before = lax.ppermute(last, axis, up)
        after = lax.ppermute(initial, axis, down)
        shard = jnp.concatenate([before, shard, after], axis=dim)
    return shard


def tap_norm(scale):
    dist = jnp.arange(-15, 16).astype(jnp.float32)
    gauss = jnp.exp(-(dist[None, :] * dist[None, :]) / (2.0 * scale[:, None] * scale[:, None]))
    return jnp.sqrt(jnp.sum(gauss * gauss, axis=1))


def tap_weight(dist, scale, norm):
    value = jnp.exp(-(dist * dist) / (2.0 * scale * scale)) / norm
    return jnp.where(jnp.abs(dist) <= 15.0, value, 0.0)


def band_matrix(scale, norm, inner, outer, offset):
    inner_pos = jnp.arange(inner).astype(jnp.float32)[:, None]
    outer_pos = jnp.arange(outer).astype(jnp.float32)[None, :]
    dist = inner_pos - offset - outer_pos
    return tap_weight(dist[None], scale[:, None, None], norm[:, None, None]).astype(jnp.bfloat16)


def slot_numbers(dest, keep, n_lon):
    hits = ((dest[:, None] == jnp.arange(n_lon, dtype=jnp.int32)[None, :]) & keep[:, None]).astype(
        jnp.int32
    )
    before = jnp.cumsum(hits, axis=0) - hits
    return jnp.sum(before * hits, axis=1)


def spread_block(part, where, width):
    cells = jnp.arange(TY * width, dtype=jnp.int32)
    grid_row = (cells // width).astype(jnp.bfloat16)
    grid_col = (cells % width).astype(jnp.bfloat16)
    onehot = (
        (where[0][:, None] == grid_row[None, :]) & (where[1][:, None] == grid_col[None, :])
    ).astype(jnp.bfloat16)
    return jnp.dot(part, onehot, preferred_element_type=jnp.float32)


def packed(innovation, owner_tile, cell_index, length_scale, eof_basis):
    n_lon = lax.axis_size("lon")
    lev, rec = innovation.shape
    cap = (2 * rec + n_lon - 1) // n_lon
    owner = owner_tile[:, 0]
    cell_row = cell_index // TX
    cell_col = cell_index % TX
    everyone = jnp.ones((rec,), jnp.bool_)
    target = owner * cap + slot_numbers(owner, everyone, n_lon)
    values = jnp.zeros((lev, n_lon * cap), jnp.bfloat16).at[:, target].set(innovation)
    coords = jnp.stack([cell_row, cell_col]).astype(jnp.bfloat16)
    places = jnp.full((2, n_lon * cap), -1.0, jnp.bfloat16).at[:, target].set(coords)
    values = values.reshape(lev, n_lon, cap)
    places = places.reshape(2, n_lon, cap)
    got_values, got_places = (
        lax.all_to_all(values, "lon", split_axis=1, concat_axis=1, tiled=True),
        lax.all_to_all(places, "lon", split_axis=1, concat_axis=1, tiled=True),
    )

    def spread_one(source, total):
        part = lax.dynamic_index_in_dim(got_values, source, 1, keepdims=False)
        where = lax.dynamic_index_in_dim(got_places, source, 1, keepdims=False)
        return total + spread_block(part, where, TX)

    summed = lax.fori_loop(0, n_lon, spread_one, jnp.zeros((lev, TY * TX), jnp.float32))
    spread = summed.astype(jnp.bfloat16).reshape(lev, TY, TX)
    padded = extended(spread, (("lon", 2),), 15)
    norm = tap_norm(length_scale)
    band_lon = band_matrix(length_scale, norm, TX + 30, TX, 15.0)
    lon_smooth = jnp.einsum(
        "cyk,ckx->cyx", padded, band_lon, preferred_element_type=jnp.float32
    ).astype(jnp.bfloat16)
    n_lat = lax.axis_size("lat")
    south = [(i, i + 1) for i in range(n_lat - 1)]
    north = [(j, i) for i, j in south]
    above = lax.ppermute(lon_smooth[:, TY - 16 :], "lat", south)
    below = lax.ppermute(lon_smooth[:, :16], "lat", north)
    column = jnp.concatenate([above, lon_smooth, below], axis=1)
    band_lat = band_matrix(length_scale, norm, TY + 32, TY, 16.0)
    smooth = jnp.einsum(
        "cky,ckx->cyx", band_lat, column, preferred_element_type=jnp.float32
    ).astype(jnp.bfloat16)
    return jnp.einsum("lc,cyx->lyx", eof_basis, smooth, preferred_element_type=jnp.float32).astype(
        jnp.bfloat16
    )


MESH = pl.DeviceIdType.MESH
HALO = 16
GROUPS = 4


def copies(ref_from, ref_to, send, recv, target):
    return pltpu.make_async_remote_copy(
        src_ref=ref_from,
        dst_ref=ref_to,
        send_sem=send,
        recv_sem=recv,
        device_id=target,
        device_id_type=MESH,
    )


def smooth_kernel(
    n_lat, innov_ref, key_ref, band_hbm, blat_ref, out_ref,
    vals, keys, picked, slots, sums, band, lon, north, south,
    band_sem, val_send, val_recv, key_send, key_recv, halo_send, halo_recv,
):
    lev, rec = innov_ref.shape
    half = rec // 2
    me = lax.axis_index("lon")
    lat = lax.axis_index("lat")
    partner = me + 1 - 2 * (me % 2)
    across = (me + 2) % 4
    far = (partner + 2) % 4
    has_up = lat > 0
    has_down = lat < n_lat - 1

    fetch = pltpu.make_async_copy(band_hbm, band, band_sem)
    fetch.start()
    barrier = pltpu.get_barrier_semaphore()
    for peer in (partner, across, far):
        pl.semaphore_signal(barrier, inc=1, device_id=(peer, lat), device_id_type=MESH)

    @pl.when(has_up)
    def _():
        pl.semaphore_signal(barrier, inc=1, device_id=(me, lat - 1), device_id_type=MESH)

    @pl.when(has_down)
    def _():
        pl.semaphore_signal(barrier, inc=1, device_id=(me, lat + 1), device_id_type=MESH)

    pl.semaphore_wait(barrier, 3 + has_up.astype(jnp.int32) + has_down.astype(jnp.int32))

    key_copies = [
        copies(key_ref, keys.at[i], key_send.at[i], key_recv.at[i], (peer, lat))
        for i, peer in enumerate((partner, across, far))
    ]
    parts = [pl.ds(0, half), pl.ds(half, half)]
    over = [
        copies(
            innov_ref.at[:, parts[h]], vals.at[1, :, parts[h]],
            val_send.at[h], val_recv.at[h], (across, lat),
        )
        for h in range(2)
    ]
    beside = copies(innov_ref, vals.at[0], val_send.at[2], val_recv.at[2], (partner, lat))
    onward = [
        copies(
            vals.at[1, :, parts[h]], vals.at[2, :, parts[h]],
            val_send.at[3 + h], val_recv.at[3 + h], (partner, lat),
        )
        for h in range(2)
    ]
    for copy in key_copies:
        copy.start()
    over[0].start()
    over[1].start()
    beside.start()

    row_of = lax.broadcasted_iota(jnp.int32, (256, rec), 0).astype(jnp.float32).astype(jnp.bfloat16)
    zero = jnp.zeros((), jnp.bfloat16)
    one = jnp.ones((), jnp.bfloat16)

    def spread(part, key, first):
        row = key >> 9
        rel = ((key & 511) - TX * me + HALO) & 511
        sub = (row & 7).astype(jnp.float32).astype(jnp.bfloat16)
        phase = row >> 3
        inside = (rel >= HALO) & (rel < HALO + TX)
        main = (phase & 1) * TX + rel - HALO
        for n in range(4):
            hit = inside & ((phase >> 1) == n)
            slots[n] = jnp.where(hit, main, -1).astype(jnp.float32)
        rim = jnp.where(rel < HALO, rel, rel - TX)
        rim_hit = (rel < HALO) | ((rel >= HALO + TX) & (rel < 2 * HALO + TX))
        slots[4] = jnp.where(rim_hit, phase * 2 * HALO + rim, -1).astype(jnp.float32)
        values = part[...]
        for t in range(8):
            mine = sub == jnp.full((), t, jnp.bfloat16)
            picked[pl.ds(t * lev, lev), :] = jnp.where(mine, values, zero)

        def tile(n, carry):
            where = slots[n].astype(jnp.bfloat16)
            onehot = jnp.where(row_of == where, one, zero)
            got = lax.dot_general(
                picked[...], onehot, (((1,), (1,)), ((), ())), preferred_element_type=jnp.float32
            )
            for side in range(2):
                piece = got[:, side * TX : (side + 1) * TX]
                if first:
                    sums[2 * n + side] = piece
                else:
                    sums[2 * n + side] += piece
            return carry

        lax.fori_loop(0, 5, tile, 0)

    spread(innov_ref, key_ref[...], True)
    key_copies[0].wait_recv()
    beside.wait_recv()
    spread(vals.at[0], keys[0], False)
    for h in range(2):
        over[h].wait_recv()
        onward[h].start()
    key_copies[1].wait_recv()
    spread(vals.at[1], keys[1], False)
    key_copies[2].wait_recv()
    for h in range(2):
        onward[h].wait_recv()
    spread(vals.at[2], keys[2], False)

    fetch.wait()
    lane = lax.broadcasted_iota(jnp.int32, (8, TX), 1) // (2 * HALO)
    width = lev // GROUPS

    def lon_one(c, carry):
        rows = pl.ds(c, 8, stride=lev)
        main = [sums[p, rows, :] for p in range(8)]
        rim = [
            jnp.where(lane == p % 4, sums[8 + p // 4, rows, :], 0.0)
            for p in range(8)
        ]
        left = jnp.concatenate(
            [jnp.concatenate(main, axis=0), jnp.concatenate(rim, axis=0)], axis=1
        ).astype(jnp.bfloat16)
        lon[c] = jnp.dot(left, band[c], preferred_element_type=jnp.float32).astype(jnp.bfloat16)
        return carry

    ups, downs = [], []
    for g in range(GROUPS):
        lax.fori_loop(g * width, (g + 1) * width, lon_one, 0, unroll=4)
        chans = pl.ds(g * width, width)
        up = copies(
            lon.at[chans, pl.ds(0, HALO), :], south.at[chans],
            halo_send.at[0, g], halo_recv.at[0, g], (me, lat - 1),
        )
        down = copies(
            lon.at[chans, pl.ds(TY - HALO, HALO), :], north.at[chans],
            halo_send.at[1, g], halo_recv.at[1, g], (me, lat + 1),
        )
        ups.append(up)
        downs.append(down)

        @pl.when(has_up)
        def _(up=up):
            up.start()

        @pl.when(has_down)
        def _(down=down):
            down.start()

    @pl.when(jnp.logical_not(has_up))
    def _():
        north[...] = jnp.zeros_like(north)

    @pl.when(jnp.logical_not(has_down))
    def _():
        south[...] = jnp.zeros_like(south)

    def lat_one(c, carry):
        column = jnp.concatenate([north[c], lon[c], south[c]], axis=0)
        out_ref[c] = jnp.dot(
            blat_ref[c], column, preferred_element_type=jnp.float32
        ).astype(jnp.bfloat16)
        return carry

    for g in range(GROUPS):

        @pl.when(has_up)
        def _(g=g):
            downs[g].wait_recv()

        @pl.when(has_down)
        def _(g=g):
            ups[g].wait_recv()

        lax.fori_loop(g * width, (g + 1) * width, lat_one, 0, unroll=4)

    for copy in key_copies + over + [beside] + onward:
        copy.wait_send()
    for g in range(GROUPS):

        @pl.when(has_up)
        def _(g=g):
            ups[g].wait_send()

        @pl.when(has_down)
        def _(g=g):
            downs[g].wait_send()


def gathered(innovation, owner_tile, cell_index, length_scale, eof_basis):
    n_lat = lax.axis_size("lat")
    lev, rec = innovation.shape
    key = ((cell_index // TX) * 512 + owner_tile[:, 0] * TX + cell_index % TX)[None, :]
    norm = tap_norm(length_scale)
    inner = jnp.arange(2 * TX, dtype=jnp.int32)
    side = (inner - TX) % (2 * HALO)
    place = jnp.where(inner < TX, inner, jnp.where(side < HALO, side - HALO, side - HALO + TX))
    dist = (place[:, None] - jnp.arange(TX, dtype=jnp.int32)[None, :]).astype(jnp.float32)
    band_lon = tap_weight(dist[None], length_scale[:, None, None], norm[:, None, None])
    dist = (
        jnp.arange(TY + 2 * HALO, dtype=jnp.int32)[None, :]
        - HALO
        - jnp.arange(TY, dtype=jnp.int32)[:, None]
    ).astype(jnp.float32)
    band_lat = tap_weight(dist[None], length_scale[:, None, None], norm[:, None, None])
    vmem = pl.BlockSpec(memory_space=pltpu.VMEM)
    smooth = pl.pallas_call(
        functools.partial(smooth_kernel, n_lat),
        out_shape=jax.ShapeDtypeStruct((lev, TY, TX), jnp.bfloat16),
        in_specs=[vmem, vmem, pl.BlockSpec(memory_space=pl.ANY), vmem],
        out_specs=vmem,
        scratch_shapes=[
            pltpu.VMEM((3, lev, rec), jnp.bfloat16),
            pltpu.VMEM((3, 1, rec), jnp.int32),
            pltpu.VMEM((8 * lev, rec), jnp.bfloat16),
            pltpu.VMEM((5, 1, rec), jnp.float32),
            pltpu.VMEM((10, 8 * lev, TX), jnp.float32),
            pltpu.VMEM((lev, 2 * TX, TX), jnp.bfloat16),
            pltpu.VMEM((lev, TY, TX), jnp.bfloat16),
            pltpu.VMEM((lev, HALO, TX), jnp.bfloat16),
            pltpu.VMEM((lev, HALO, TX), jnp.bfloat16),
            pltpu.SemaphoreType.DMA,
            pltpu.SemaphoreType.DMA((5,)),
            pltpu.SemaphoreType.DMA((5,)),
            pltpu.SemaphoreType.DMA((3,)),
            pltpu.SemaphoreType.DMA((3,)),
            pltpu.SemaphoreType.DMA((2, GROUPS)),
            pltpu.SemaphoreType.DMA((2, GROUPS)),
        ],
        compiler_params=pltpu.CompilerParams(
            collective_id=0, has_side_effects=True, vmem_limit_bytes=40 * 1024 * 1024
        ),
        cost_estimate=pl.CostEstimate(
            flops=2 * 8 * lev * 4 * rec * 1280, bytes_accessed=8 * 1024 * 1024, transcendentals=0
        ),
    )(innovation, key, band_lon.astype(jnp.bfloat16), band_lat.astype(jnp.bfloat16))
    return jnp.einsum("lc,cyx->lyx", eof_basis, smooth, preferred_element_type=jnp.float32).astype(
        jnp.bfloat16
    )


def solution(mesh):
    in_specs = (P(None, ("lon", "lat")), P(("lon", "lat"), None), P(("lon", "lat")), P(), P())
    out_specs = P(None, "lat", "lon")
    local = gathered if mesh.shape["lon"] == 4 else packed
    return jax.shard_map(local, mesh=mesh, in_specs=in_specs, out_specs=out_specs, check_vma=False)
```

```python
import functools

import jax
import jax.numpy as jnp
from jax import lax
from jax.experimental import pallas as pl
from jax.experimental.pallas import tpu as pltpu
from jax.sharding import PartitionSpec as P

TX = 128
TY = 64


def extended(shard, sides, width):
    for axis, dim in sides:
        size, length = (lax.axis_size(axis), shard.shape[dim])
        up = [(i, (i + 1) % size) for i in range(size)]
        down = [(j, i) for i, j in up]
        last = lax.slice_in_dim(shard, length - width, length, axis=dim)
        initial = lax.slice_in_dim(shard, 0, width, axis=dim)
        before = lax.ppermute(last, axis, up)
        after = lax.ppermute(initial, axis, down)
        shard = jnp.concatenate([before, shard, after], axis=dim)
    return shard


def tap_norm(scale):
    dist = jnp.arange(-15, 16).astype(jnp.float32)
    gauss = jnp.exp(-(dist[None, :] * dist[None, :]) / (2.0 * scale[:, None] * scale[:, None]))
    return jnp.sqrt(jnp.sum(gauss * gauss, axis=1))


def tap_weight(dist, scale, norm):
    value = jnp.exp(-(dist * dist) / (2.0 * scale * scale)) / norm
    return jnp.where(jnp.abs(dist) <= 15.0, value, 0.0)


def band_matrix(scale, norm, inner, outer, offset):
    inner_pos = jnp.arange(inner).astype(jnp.float32)[:, None]
    outer_pos = jnp.arange(outer).astype(jnp.float32)[None, :]
    dist = inner_pos - offset - outer_pos
    return tap_weight(dist[None], scale[:, None, None], norm[:, None, None]).astype(jnp.bfloat16)


def slot_numbers(dest, keep, n_lon):
    hits = ((dest[:, None] == jnp.arange(n_lon, dtype=jnp.int32)[None, :]) & keep[:, None]).astype(
        jnp.int32
    )
    before = jnp.cumsum(hits, axis=0) - hits
    return jnp.sum(before * hits, axis=1)


def spread_block(part, where, width):
    cells = jnp.arange(TY * width, dtype=jnp.int32)
    grid_row = (cells // width).astype(jnp.bfloat16)
    grid_col = (cells % width).astype(jnp.bfloat16)
    onehot = (
        (where[0][:, None] == grid_row[None, :]) & (where[1][:, None] == grid_col[None, :])
    ).astype(jnp.bfloat16)
    return jnp.dot(part, onehot, preferred_element_type=jnp.float32)


def packed(innovation, owner_tile, cell_index, length_scale, eof_basis):
    n_lon = lax.axis_size("lon")
    lev, rec = innovation.shape
    cap = (2 * rec + n_lon - 1) // n_lon
    owner = owner_tile[:, 0]
    cell_row = cell_index // TX
    cell_col = cell_index % TX
    everyone = jnp.ones((rec,), jnp.bool_)
    target = owner * cap + slot_numbers(owner, everyone, n_lon)
    values = jnp.zeros((lev, n_lon * cap), jnp.bfloat16).at[:, target].set(innovation)
    coords = jnp.stack([cell_row, cell_col]).astype(jnp.bfloat16)
    places = jnp.full((2, n_lon * cap), -1.0, jnp.bfloat16).at[:, target].set(coords)
    values = values.reshape(lev, n_lon, cap)
    places = places.reshape(2, n_lon, cap)
    got_values, got_places = (
        lax.all_to_all(values, "lon", split_axis=1, concat_axis=1, tiled=True),
        lax.all_to_all(places, "lon", split_axis=1, concat_axis=1, tiled=True),
    )

    def spread_one(source, total):
        part = lax.dynamic_index_in_dim(got_values, source, 1, keepdims=False)
        where = lax.dynamic_index_in_dim(got_places, source, 1, keepdims=False)
        return total + spread_block(part, where, TX)

    summed = lax.fori_loop(0, n_lon, spread_one, jnp.zeros((lev, TY * TX), jnp.float32))
    spread = summed.astype(jnp.bfloat16).reshape(lev, TY, TX)
    padded = extended(spread, (("lon", 2),), 15)
    norm = tap_norm(length_scale)
    band_lon = band_matrix(length_scale, norm, TX + 30, TX, 15.0)
    lon_smooth = jnp.einsum(
        "cyk,ckx->cyx", padded, band_lon, preferred_element_type=jnp.float32
    ).astype(jnp.bfloat16)
    n_lat = lax.axis_size("lat")
    south = [(i, i + 1) for i in range(n_lat - 1)]
    north = [(j, i) for i, j in south]
    above = lax.ppermute(lon_smooth[:, TY - 16 :], "lat", south)
    below = lax.ppermute(lon_smooth[:, :16], "lat", north)
    column = jnp.concatenate([above, lon_smooth, below], axis=1)
    band_lat = band_matrix(length_scale, norm, TY + 32, TY, 16.0)
    smooth = jnp.einsum(
        "cky,ckx->cyx", band_lat, column, preferred_element_type=jnp.float32
    ).astype(jnp.bfloat16)
    return jnp.einsum("lc,cyx->lyx", eof_basis, smooth, preferred_element_type=jnp.float32).astype(
        jnp.bfloat16
    )


MESH = pl.DeviceIdType.MESH
HALO = 16
GROUPS = 4


def copies(ref_from, ref_to, send, recv, target):
    return pltpu.make_async_remote_copy(
        src_ref=ref_from,
        dst_ref=ref_to,
        send_sem=send,
        recv_sem=recv,
        device_id=target,
        device_id_type=MESH,
    )


def smooth_kernel(
    n_lat, innov_ref, owner_ref, cell_ref, scale_ref, out_ref,
    key_ref, vals, keys, picked, slots, sums, weights, band, lon, north, south,
    val_send, val_recv, key_send, key_recv, halo_send, halo_recv,
):
    lev, rec = innov_ref.shape
    half = rec // 2
    me = lax.axis_index("lon")
    lat = lax.axis_index("lat")
    partner = me + 1 - 2 * (me % 2)
    across = (me + 2) % 4
    far = (partner + 2) % 4
    has_up = lat > 0
    has_down = lat < n_lat - 1

    barrier = pltpu.get_barrier_semaphore()
    for peer in (partner, across, far):
        pl.semaphore_signal(barrier, inc=1, device_id=(peer, lat), device_id_type=MESH)

    @pl.when(has_up)
    def _():
        pl.semaphore_signal(barrier, inc=1, device_id=(me, lat - 1), device_id_type=MESH)

    @pl.when(has_down)
    def _():
        pl.semaphore_signal(barrier, inc=1, device_id=(me, lat + 1), device_id_type=MESH)

    cell = cell_ref[...]
    key_ref[...] = (cell >> 7) * 512 + owner_ref[...] * TX + (cell & (TX - 1))
    pl.semaphore_wait(barrier, 3 + has_up.astype(jnp.int32) + has_down.astype(jnp.int32))

    key_copies = [
        copies(key_ref, keys.at[i], key_send.at[i], key_recv.at[i], (peer, lat))
        for i, peer in enumerate((partner, across, far))
    ]
    parts = [pl.ds(0, half), pl.ds(half, half)]
    over = [
        copies(
            innov_ref.at[:, parts[h]], vals.at[1, :, parts[h]],
            val_send.at[h], val_recv.at[h], (across, lat),
        )
        for h in range(2)
    ]
    beside = copies(innov_ref, vals.at[0], val_send.at[2], val_recv.at[2], (partner, lat))
    onward = [
        copies(
            vals.at[1, :, parts[h]], vals.at[2, :, parts[h]],
            val_send.at[3 + h], val_recv.at[3 + h], (partner, lat),
        )
        for h in range(2)
    ]
    for copy in key_copies:
        copy.start()
    over[0].start()
    over[1].start()
    beside.start()

    row_of = lax.broadcasted_iota(jnp.int32, (256, rec), 0).astype(jnp.float32).astype(jnp.bfloat16)
    zero = jnp.zeros((), jnp.bfloat16)
    one = jnp.ones((), jnp.bfloat16)

    def sort_out(part, key, at):
        row = key >> 9
        rel = ((key & 511) - TX * me + HALO) & 511
        sub = (row & 7).astype(jnp.float32).astype(jnp.bfloat16)
        phase = row >> 3
        inside = (rel >= HALO) & (rel < HALO + TX)
        main = (phase & 1) * TX + rel - HALO
        for n, pair in ((0, 0), (1, 3), (3, 1), (4, 2)):
            hit = inside & ((phase >> 1) == pair)
            slots[at, n] = jnp.where(hit, main, -1).astype(jnp.float32)
        rim = jnp.where(rel < HALO, rel, rel - TX)
        rim_hit = (rel < HALO) | ((rel >= HALO + TX) & (rel < 2 * HALO + TX))
        slots[at, 2] = jnp.where(rim_hit, phase * 2 * HALO + rim, -1).astype(jnp.float32)
        values = part[...]
        for t in range(8):
            mine = sub == jnp.full((), t, jnp.bfloat16)
            picked[at, pl.ds(t * lev, lev), :] = jnp.where(mine, values, zero)

    def spread(blocks, tiles, first=False):
        def tile(n, carry):
            got = None
            for at in blocks:
                where = slots[at, n].astype(jnp.bfloat16)
                onehot = jnp.where(row_of == where, one, zero)
                term = lax.dot_general(
                    picked[at], onehot, (((1,), (1,)), ((), ())),
                    preferred_element_type=jnp.float32,
                )
                got = term if got is None else got + term
            for side in range(2):
                piece = got[:, side * TX : (side + 1) * TX]
                if first:
                    sums[2 * n + side] = piece
                else:
                    sums[2 * n + side] += piece
            return carry

        lax.fori_loop(tiles[0], tiles[1], tile, 0)

    sort_out(innov_ref, key_ref[...], 0)
    spread([0], (0, 5), True)

    line = lax.broadcasted_iota(jnp.int32, (lev, TX), 1)
    near = jnp.where(line < TX // 2, line, line - TX).astype(jnp.float32)
    scale = scale_ref[...]
    gauss = jnp.where(
        jnp.abs(near) <= 15.0, jnp.exp(-(near * near) / (2.0 * scale * scale)), 0.0
    )
    norm = jnp.sqrt(jnp.sum(gauss * gauss, axis=1, keepdims=True))
    weights[...] = gauss / norm
    down_at = lax.broadcasted_iota(jnp.int32, (TX, TX), 0)
    side_at = lax.broadcasted_iota(jnp.int32, (TX, TX), 1)
    straight = jnp.abs(down_at - side_at) < TX // 2
    west = side_at[:HALO] < TX // 2

    def band_one(c, carry):
        ring = pltpu.roll(
            jnp.broadcast_to(weights[pl.ds(c, 1), :], (TX, TX)), 0, 1, stride=1, stride_axis=0
        )
        band[c, :TX] = jnp.where(straight, ring, 0.0).astype(jnp.bfloat16)
        rim = jnp.concatenate(
            [jnp.where(west, ring[TX - HALO :], 0.0), jnp.where(west, 0.0, ring[:HALO])], axis=0
        ).astype(jnp.bfloat16)
        for t in range(4):
            band[c, TX + 2 * HALO * t : TX + 2 * HALO * (t + 1)] = rim
        return carry

    lax.fori_loop(0, lev, band_one, 0, unroll=4)

    key_copies[0].wait_recv()
    beside.wait_recv()
    sort_out(vals.at[0], keys[0], 0)
    spread([0], (0, 5))
    for h in range(2):
        over[h].wait_recv()
        onward[h].start()
    key_copies[1].wait_recv()
    sort_out(vals.at[1], keys[1], 0)
    key_copies[2].wait_recv()
    for h in range(2):
        onward[h].wait_recv()
    sort_out(vals.at[2], keys[2], 1)
    spread([0, 1], (0, 3))

    lane = lax.broadcasted_iota(jnp.int32, (8, TX), 1) // (2 * HALO)
    width = lev // GROUPS
    spot = (0, 1, 6, 7, 8, 9, 2, 3)

    def lon_rows(c, phases):
        rows = pl.ds(c, 8, stride=lev)
        main = [sums[spot[p], rows, :] for p in phases]
        rim = [jnp.where(lane == p % 4, sums[4 + p // 4, rows, :], 0.0) for p in phases]
        left = jnp.concatenate(
            [jnp.concatenate(main, axis=0), jnp.concatenate(rim, axis=0)], axis=1
        ).astype(jnp.bfloat16)
        return jnp.dot(left, band[c], preferred_element_type=jnp.float32).astype(jnp.bfloat16)

    def lon_one(c, carry):
        got = lon_rows(c, (0, 1, 6, 7))
        lon[c, :HALO] = got[:HALO]
        lon[c, TY - HALO :] = got[HALO:]
        return carry

    def mid_one(c, carry):
        lon[c, HALO : TY - HALO] = lon_rows(c, (2, 3, 4, 5))
        return carry

    def inner_one(c, carry):
        out_ref[c, HALO : TY - HALO] = jnp.dot(
            band[c, HALO : TY - HALO, :TY], lon[c], preferred_element_type=jnp.float32
        ).astype(jnp.bfloat16)
        return carry

    ups, downs = [], []
    for g in range(GROUPS):
        lax.fori_loop(g * width, (g + 1) * width, lon_one, 0, unroll=4)
        chans = pl.ds(g * width, width)
        up = copies(
            lon.at[chans, pl.ds(0, HALO), :], south.at[chans],
            halo_send.at[0, g], halo_recv.at[0, g], (me, lat - 1),
        )
        down = copies(
            lon.at[chans, pl.ds(TY - HALO, HALO), :], north.at[chans],
            halo_send.at[1, g], halo_recv.at[1, g], (me, lat + 1),
        )
        ups.append(up)
        downs.append(down)

        @pl.when(has_up)
        def _(up=up):
            up.start()

        @pl.when(has_down)
        def _(down=down):
            down.start()

    @pl.when(jnp.logical_not(has_up))
    def _():
        north[...] = jnp.zeros_like(north)

    @pl.when(jnp.logical_not(has_down))
    def _():
        south[...] = jnp.zeros_like(south)

    spread([0, 1], (3, 5))
    lax.fori_loop(0, lev, mid_one, 0, unroll=4)
    lax.fori_loop(0, lev, inner_one, 0, unroll=4)

    def lat_one(c, carry):
        own = lon[c]
        column = jnp.concatenate(
            [
                jnp.concatenate([north[c], own[: 2 * HALO]], axis=0),
                jnp.concatenate([own[TY - 2 * HALO :], south[c]], axis=0),
            ],
            axis=1,
        )
        got = jnp.dot(
            band[c, HALO : 2 * HALO, : 3 * HALO], column, preferred_element_type=jnp.float32
        ).astype(jnp.bfloat16)
        out_ref[c, :HALO] = got[:, :TX]
        out_ref[c, TY - HALO :] = got[:, TX:]
        return carry

    for g in range(GROUPS):

        @pl.when(has_up)
        def _(g=g):
            downs[g].wait_recv()

        @pl.when(has_down)
        def _(g=g):
            ups[g].wait_recv()

        lax.fori_loop(g * width, (g + 1) * width, lat_one, 0, unroll=4)

    for copy in key_copies + over + [beside] + onward:
        copy.wait_send()
    for g in range(GROUPS):

        @pl.when(has_up)
        def _(g=g):
            ups[g].wait_send()

        @pl.when(has_down)
        def _(g=g):
            downs[g].wait_send()


def mix_kernel(eof_ref, field_ref, out_ref, wide):
    levels, lev = eof_ref.shape

    @pl.when(pl.program_id(0) == 0)
    def _():
        copy_of = lax.broadcasted_iota(jnp.int32, (lev, 8 * lev), 1) // 8
        chan = lax.broadcasted_iota(jnp.int32, (lev, 8 * lev), 0)
        across = jnp.where(copy_of == chan, 1.0, 0.0).astype(jnp.bfloat16)
        flat = jnp.dot(eof_ref[...], across, preferred_element_type=jnp.float32)
        row = lax.broadcasted_iota(jnp.int32, (8 * levels, levels), 0) // 8
        level = lax.broadcasted_iota(jnp.int32, (8 * levels, levels), 1)
        down = jnp.where(row == level, 1.0, 0.0).astype(jnp.bfloat16)
        tall = jnp.dot(down, flat.astype(jnp.bfloat16), preferred_element_type=jnp.float32)
        y_out = lax.broadcasted_iota(jnp.int32, (8 * levels, 8 * lev), 0) % 8
        y_in = lax.broadcasted_iota(jnp.int32, (8 * levels, 8 * lev), 1) % 8
        wide[...] = jnp.where(y_out == y_in, tall, 0.0).astype(jnp.bfloat16)

    field = field_ref[...].astype(jnp.float32)
    right = jnp.concatenate(
        [field[:, :8].reshape(8 * lev, TX), field[:, 8:].reshape(8 * lev, TX)], axis=1
    ).astype(jnp.bfloat16)
    got = jnp.dot(wide[...], right, preferred_element_type=jnp.float32)
    out_ref[...] = jnp.concatenate(
        [got[:, :TX].reshape(levels, 8, TX), got[:, TX:].reshape(levels, 8, TX)], axis=1
    ).astype(jnp.bfloat16)


def gathered(innovation, owner_tile, cell_index, length_scale, eof_basis):
    n_lat = lax.axis_size("lat")
    lev, rec = innovation.shape
    levels = eof_basis.shape[0]
    scale = jnp.broadcast_to(length_scale[:, None], (lev, TX))
    vmem = pl.BlockSpec(memory_space=pltpu.VMEM)
    smooth = pl.pallas_call(
        functools.partial(smooth_kernel, n_lat),
        out_shape=jax.ShapeDtypeStruct((lev, TY, TX), jnp.bfloat16),
        in_specs=[vmem] * 4,
        out_specs=vmem,
        scratch_shapes=[
            pltpu.VMEM((1, rec), jnp.int32),
            pltpu.VMEM((3, lev, rec), jnp.bfloat16),
            pltpu.VMEM((3, 1, rec), jnp.int32),
            pltpu.VMEM((2, 8 * lev, rec), jnp.bfloat16),
            pltpu.VMEM((2, 5, 1, rec), jnp.float32),
            pltpu.VMEM((10, 8 * lev, TX), jnp.float32),
            pltpu.VMEM((lev, TX), jnp.float32),
            pltpu.VMEM((lev, 2 * TX, TX), jnp.bfloat16),
            pltpu.VMEM((lev, TY, TX), jnp.bfloat16),
            pltpu.VMEM((lev, HALO, TX), jnp.bfloat16),
            pltpu.VMEM((lev, HALO, TX), jnp.bfloat16),
            pltpu.SemaphoreType.DMA((5,)),
            pltpu.SemaphoreType.DMA((5,)),
            pltpu.SemaphoreType.DMA((3,)),
            pltpu.SemaphoreType.DMA((3,)),
            pltpu.SemaphoreType.DMA((2, GROUPS)),
            pltpu.SemaphoreType.DMA((2, GROUPS)),
        ],
        compiler_params=pltpu.CompilerParams(
            collective_id=0, has_side_effects=True, vmem_limit_bytes=40 * 1024 * 1024
        ),
        cost_estimate=pl.CostEstimate(
            flops=2 * 8 * lev * 4 * rec * 1280, bytes_accessed=8 * 1024 * 1024, transcendentals=0
        ),
    )(innovation, owner_tile.reshape(1, rec), cell_index.reshape(1, rec), scale)
    return pl.pallas_call(
        mix_kernel,
        out_shape=jax.ShapeDtypeStruct((levels, TY, TX), jnp.bfloat16),
        grid=(TY // 16,),
        in_specs=[
            pl.BlockSpec((levels, lev), lambda g: (0, 0)),
            pl.BlockSpec((lev, 16, TX), lambda g: (0, g, 0)),
        ],
        out_specs=pl.BlockSpec((levels, 16, TX), lambda g: (0, g, 0)),
        scratch_shapes=[pltpu.VMEM((8 * levels, 8 * lev), jnp.bfloat16)],
        compiler_params=pltpu.CompilerParams(vmem_limit_bytes=40 * 1024 * 1024),
    )(eof_basis, smooth)


def solution(mesh):
    in_specs = (P(None, ("lon", "lat")), P(("lon", "lat"), None), P(("lon", "lat")), P(), P())
    out_specs = P(None, "lat", "lon")
    local = gathered if mesh.shape["lon"] == 4 else packed
    return jax.shard_map(local, mesh=mesh, in_specs=in_specs, out_specs=out_specs, check_vma=False)
```

```python
import functools

import jax
import jax.numpy as jnp
from jax import lax
from jax.experimental import pallas as pl
from jax.experimental.pallas import tpu as pltpu
from jax.sharding import PartitionSpec as P

TX = 128
TY = 64


def extended(shard, sides, width):
    for axis, dim in sides:
        size, length = (lax.axis_size(axis), shard.shape[dim])
        up = [(i, (i + 1) % size) for i in range(size)]
        down = [(j, i) for i, j in up]
        last = lax.slice_in_dim(shard, length - width, length, axis=dim)
        initial = lax.slice_in_dim(shard, 0, width, axis=dim)
        before = lax.ppermute(last, axis, up)
        after = lax.ppermute(initial, axis, down)
        shard = jnp.concatenate([before, shard, after], axis=dim)
    return shard


def tap_norm(scale):
    dist = jnp.arange(-15, 16).astype(jnp.float32)
    gauss = jnp.exp(-(dist[None, :] * dist[None, :]) / (2.0 * scale[:, None] * scale[:, None]))
    return jnp.sqrt(jnp.sum(gauss * gauss, axis=1))


def tap_weight(dist, scale, norm):
    value = jnp.exp(-(dist * dist) / (2.0 * scale * scale)) / norm
    return jnp.where(jnp.abs(dist) <= 15.0, value, 0.0)


def band_matrix(scale, norm, inner, outer, offset):
    inner_pos = jnp.arange(inner).astype(jnp.float32)[:, None]
    outer_pos = jnp.arange(outer).astype(jnp.float32)[None, :]
    dist = inner_pos - offset - outer_pos
    return tap_weight(dist[None], scale[:, None, None], norm[:, None, None]).astype(jnp.bfloat16)


def slot_numbers(dest, keep, n_lon):
    hits = ((dest[:, None] == jnp.arange(n_lon, dtype=jnp.int32)[None, :]) & keep[:, None]).astype(
        jnp.int32
    )
    before = jnp.cumsum(hits, axis=0) - hits
    return jnp.sum(before * hits, axis=1)


def spread_block(part, where, width):
    cells = jnp.arange(TY * width, dtype=jnp.int32)
    grid_row = (cells // width).astype(jnp.bfloat16)
    grid_col = (cells % width).astype(jnp.bfloat16)
    onehot = (
        (where[0][:, None] == grid_row[None, :]) & (where[1][:, None] == grid_col[None, :])
    ).astype(jnp.bfloat16)
    return jnp.dot(part, onehot, preferred_element_type=jnp.float32)


def packed(innovation, owner_tile, cell_index, length_scale, eof_basis):
    n_lon = lax.axis_size("lon")
    lev, rec = innovation.shape
    cap = (2 * rec + n_lon - 1) // n_lon
    owner = owner_tile[:, 0]
    cell_row = cell_index // TX
    cell_col = cell_index % TX
    everyone = jnp.ones((rec,), jnp.bool_)
    target = owner * cap + slot_numbers(owner, everyone, n_lon)
    values = jnp.zeros((lev, n_lon * cap), jnp.bfloat16).at[:, target].set(innovation)
    coords = jnp.stack([cell_row, cell_col]).astype(jnp.bfloat16)
    places = jnp.full((2, n_lon * cap), -1.0, jnp.bfloat16).at[:, target].set(coords)
    values = values.reshape(lev, n_lon, cap)
    places = places.reshape(2, n_lon, cap)
    got_values, got_places = (
        lax.all_to_all(values, "lon", split_axis=1, concat_axis=1, tiled=True),
        lax.all_to_all(places, "lon", split_axis=1, concat_axis=1, tiled=True),
    )

    def spread_one(source, total):
        part = lax.dynamic_index_in_dim(got_values, source, 1, keepdims=False)
        where = lax.dynamic_index_in_dim(got_places, source, 1, keepdims=False)
        return total + spread_block(part, where, TX)

    summed = lax.fori_loop(0, n_lon, spread_one, jnp.zeros((lev, TY * TX), jnp.float32))
    spread = summed.astype(jnp.bfloat16).reshape(lev, TY, TX)
    padded = extended(spread, (("lon", 2),), 15)
    norm = tap_norm(length_scale)
    band_lon = band_matrix(length_scale, norm, TX + 30, TX, 15.0)
    lon_smooth = jnp.einsum(
        "cyk,ckx->cyx", padded, band_lon, preferred_element_type=jnp.float32
    ).astype(jnp.bfloat16)
    n_lat = lax.axis_size("lat")
    south = [(i, i + 1) for i in range(n_lat - 1)]
    north = [(j, i) for i, j in south]
    above = lax.ppermute(lon_smooth[:, TY - 16 :], "lat", south)
    below = lax.ppermute(lon_smooth[:, :16], "lat", north)
    column = jnp.concatenate([above, lon_smooth, below], axis=1)
    band_lat = band_matrix(length_scale, norm, TY + 32, TY, 16.0)
    smooth = jnp.einsum(
        "cky,ckx->cyx", band_lat, column, preferred_element_type=jnp.float32
    ).astype(jnp.bfloat16)
    return jnp.einsum("lc,cyx->lyx", eof_basis, smooth, preferred_element_type=jnp.float32).astype(
        jnp.bfloat16
    )


MESH = pl.DeviceIdType.MESH
HALO = 16
GROUPS = 4


def copies(ref_from, ref_to, send, recv, target):
    return pltpu.make_async_remote_copy(
        src_ref=ref_from,
        dst_ref=ref_to,
        send_sem=send,
        recv_sem=recv,
        device_id=target,
        device_id_type=MESH,
    )


def smooth_kernel(
    n_lat, innov_hbm, owner_hbm, cell_hbm, scale_hbm, eof_hbm, out_hbm, wide_hbm,
    out_ref, wide_ref, store,
    innov_ref, owner_ref, cell_ref, scale_ref, eof_ref, load, key_ref, vals, keys, picked, slots, sums, weights, band, lon, north, south,
    val_send, val_recv, key_send, key_recv, halo_send, halo_recv,
):
    lev, rec = innov_ref.shape
    levels = eof_ref.shape[1]
    loads = [
        pltpu.make_async_copy(there, here, load.at[i])
        for i, (there, here) in enumerate(
            (
                (owner_hbm, owner_ref),
                (cell_hbm, cell_ref),
                (innov_hbm, innov_ref),
                (scale_hbm, scale_ref),
                (eof_hbm, eof_ref),
            )
        )
    ]
    for copy in loads:
        copy.start()
    half = rec // 2
    me = lax.axis_index("lon")
    lat = lax.axis_index("lat")
    partner = me + 1 - 2 * (me % 2)
    across = (me + 2) % 4
    far = (partner + 2) % 4
    has_up = lat > 0
    has_down = lat < n_lat - 1

    barrier = pltpu.get_barrier_semaphore()
    for peer in (partner, across, far):
        pl.semaphore_signal(barrier, inc=1, device_id=(peer, lat), device_id_type=MESH)

    @pl.when(has_up)
    def _():
        pl.semaphore_signal(barrier, inc=1, device_id=(me, lat - 1), device_id_type=MESH)

    @pl.when(has_down)
    def _():
        pl.semaphore_signal(barrier, inc=1, device_id=(me, lat + 1), device_id_type=MESH)

    loads[0].wait()
    loads[1].wait()
    cell = cell_ref[...].reshape(1, rec)
    key_ref[...] = (cell >> 7) * 512 + owner_ref[...] * TX + (cell & (TX - 1))
    pl.semaphore_wait(barrier, 3 + has_up.astype(jnp.int32) + has_down.astype(jnp.int32))

    key_copies = [
        copies(key_ref, keys.at[i], key_send.at[i], key_recv.at[i], (peer, lat))
        for i, peer in enumerate((partner, across, far))
    ]
    parts = [pl.ds(0, half), pl.ds(half, half)]
    over = [
        copies(
            innov_hbm.at[:, parts[h]], vals.at[1, :, parts[h]],
            val_send.at[h], val_recv.at[h], (across, lat),
        )
        for h in range(2)
    ]
    beside = copies(innov_hbm, vals.at[0], val_send.at[2], val_recv.at[2], (partner, lat))
    onward = [
        copies(
            vals.at[1, :, parts[h]], vals.at[2, :, parts[h]],
            val_send.at[3 + h], val_recv.at[3 + h], (partner, lat),
        )
        for h in range(2)
    ]
    for copy in key_copies:
        copy.start()
    over[0].start()
    over[1].start()
    beside.start()

    row_of = lax.broadcasted_iota(jnp.int32, (256, rec), 0).astype(jnp.float32).astype(jnp.bfloat16)
    zero = jnp.zeros((), jnp.bfloat16)
    one = jnp.ones((), jnp.bfloat16)

    def sort_out(part, key, at):
        row = key >> 9
        rel = ((key & 511) - TX * me + HALO) & 511
        sub = (row & 7).astype(jnp.float32).astype(jnp.bfloat16)
        phase = row >> 3
        inside = (rel >= HALO) & (rel < HALO + TX)
        main = (phase & 1) * TX + rel - HALO
        for n, pair in ((0, 0), (1, 3), (3, 1), (4, 2)):
            hit = inside & ((phase >> 1) == pair)
            slots[at, n] = jnp.where(hit, main, -1).astype(jnp.float32)
        rim = jnp.where(rel < HALO, rel, rel - TX)
        rim_hit = (rel < HALO) | ((rel >= HALO + TX) & (rel < 2 * HALO + TX))
        slots[at, 2] = jnp.where(rim_hit, phase * 2 * HALO + rim, -1).astype(jnp.float32)
        values = part[...]
        for t in range(8):
            mine = sub == jnp.full((), t, jnp.bfloat16)
            picked[at, pl.ds(t * lev, lev), :] = jnp.where(mine, values, zero)

    def spread(blocks, tiles, first=False):
        def tile(n, carry):
            got = None
            for at in blocks:
                where = slots[at, n].astype(jnp.bfloat16)
                onehot = jnp.where(row_of == where, one, zero)
                term = lax.dot_general(
                    picked[at], onehot, (((1,), (1,)), ((), ())),
                    preferred_element_type=jnp.float32,
                )
                got = term if got is None else got + term
            for side in range(2):
                piece = got[:, side * TX : (side + 1) * TX]
                if first:
                    sums[2 * n + side] = piece
                else:
                    sums[2 * n + side] += piece
            return carry

        lax.fori_loop(tiles[0], tiles[1], tile, 0)

    loads[2].wait()
    sort_out(innov_ref, key_ref[...], 0)
    spread([0], (0, 3), True)

    line = lax.broadcasted_iota(jnp.int32, (lev, TX), 1)
    near = jnp.where(line < TX // 2, line, line - TX).astype(jnp.float32)
    loads[3].wait()
    diagonal = lax.broadcasted_iota(jnp.int32, (lev, lev), 0) == lax.broadcasted_iota(
        jnp.int32, (lev, lev), 1
    )
    scale = jnp.sum(
        jnp.where(diagonal, jnp.broadcast_to(scale_ref[...], (lev, lev)), 0.0), axis=1, keepdims=True
    )
    gauss = jnp.where(
        jnp.abs(near) <= 15.0, jnp.exp(-(near * near) / (2.0 * scale * scale)), 0.0
    )
    norm = jnp.sqrt(jnp.sum(gauss * gauss, axis=1, keepdims=True))
    weights[...] = gauss / norm
    down_at = lax.broadcasted_iota(jnp.int32, (TX, TX), 0)
    side_at = lax.broadcasted_iota(jnp.int32, (TX, TX), 1)
    straight = jnp.abs(down_at - side_at) < TX // 2
    west = side_at[:HALO] < TX // 2

    def band_one(c, carry):
        ring = pltpu.roll(
            jnp.broadcast_to(weights[pl.ds(c, 1), :], (TX, TX)), 0, 1, stride=1, stride_axis=0
        )
        band[c, :TX] = jnp.where(straight, ring, 0.0).astype(jnp.bfloat16)
        rim = jnp.concatenate(
            [jnp.where(west, ring[TX - HALO :], 0.0), jnp.where(west, 0.0, ring[:HALO])], axis=0
        ).astype(jnp.bfloat16)
        for t in range(4):
            band[c, TX + 2 * HALO * t : TX + 2 * HALO * (t + 1)] = rim
        return carry

    lax.fori_loop(0, lev, band_one, 0, unroll=4)

    key_copies[0].wait_recv()
    beside.wait_recv()
    sort_out(vals.at[0], keys[0], 1)
    spread([1], (0, 3))
    for h in range(2):
        over[h].wait_recv()
        onward[h].start()
    key_copies[1].wait_recv()
    sort_out(vals.at[1], keys[1], 2)
    spread([2], (0, 3))
    key_copies[2].wait_recv()
    for h in range(2):
        onward[h].wait_recv()
    sort_out(vals.at[2], keys[2], 3)
    spread([3], (0, 3))

    lane = lax.broadcasted_iota(jnp.int32, (8, TX), 1) // (2 * HALO)
    width = lev // GROUPS
    spot = (0, 1, 6, 7, 8, 9, 2, 3)

    def lon_rows(c, phases):
        rows = pl.ds(c, 8, stride=lev)
        main = [sums[spot[p], rows, :] for p in phases]
        rim = [jnp.where(lane == p % 4, sums[4 + p // 4, rows, :], 0.0) for p in phases]
        left = jnp.concatenate(
            [jnp.concatenate(main, axis=0), jnp.concatenate(rim, axis=0)], axis=1
        ).astype(jnp.bfloat16)
        return jnp.dot(left, band[c], preferred_element_type=jnp.float32).astype(jnp.bfloat16)

    def lon_one(c, carry):
        got = lon_rows(c, (0, 1, 6, 7))
        lon[c, :HALO] = got[:HALO]
        lon[c, TY - HALO :] = got[HALO:]
        return carry

    def mid_one(c, carry):
        lon[c, HALO : TY - HALO] = lon_rows(c, (2, 3, 4, 5))
        return carry

    def inner_one(c, carry):
        out_ref[c, HALO : TY - HALO] = jnp.dot(
            band[c, HALO : TY - HALO, :TY], lon[c], preferred_element_type=jnp.float32
        ).astype(jnp.bfloat16)
        return carry

    ups, downs = [], []
    for g in range(GROUPS):
        lax.fori_loop(g * width, (g + 1) * width, lon_one, 0, unroll=4)
        chans = pl.ds(g * width, width)
        up = copies(
            lon.at[chans, pl.ds(0, HALO), :], south.at[chans],
            halo_send.at[0, g], halo_recv.at[0, g], (me, lat - 1),
        )
        down = copies(
            lon.at[chans, pl.ds(TY - HALO, HALO), :], north.at[chans],
            halo_send.at[1, g], halo_recv.at[1, g], (me, lat + 1),
        )
        ups.append(up)
        downs.append(down)

        @pl.when(has_up)
        def _(up=up):
            up.start()

        @pl.when(has_down)
        def _(down=down):
            down.start()

    @pl.when(jnp.logical_not(has_up))
    def _():
        north[...] = jnp.zeros_like(north)

    @pl.when(jnp.logical_not(has_down))
    def _():
        south[...] = jnp.zeros_like(south)

    spread([0, 1, 2, 3], (3, 5), True)
    lax.fori_loop(0, lev, mid_one, 0, unroll=4)
    lax.fori_loop(0, lev, inner_one, 0, unroll=4)

    loads[4].wait()
    copy_of = lax.broadcasted_iota(jnp.int32, (lev, 8 * lev), 1) // 8
    chan = lax.broadcasted_iota(jnp.int32, (lev, 8 * lev), 0)
    repeat = jnp.where(copy_of == chan, 1.0, 0.0).astype(jnp.bfloat16)
    flat = lax.dot_general(
        eof_ref[...], repeat, (((0,), (0,)), ((), ())), preferred_element_type=jnp.float32
    ).astype(jnp.bfloat16)
    row = lax.broadcasted_iota(jnp.int32, (8 * levels, levels), 0) // 8
    level = lax.broadcasted_iota(jnp.int32, (8 * levels, levels), 1)
    down_all = jnp.where(row == level, 1.0, 0.0).astype(jnp.bfloat16)
    tall = jnp.dot(down_all, flat, preferred_element_type=jnp.float32)
    y_out = lax.broadcasted_iota(jnp.int32, (8 * levels, 8 * lev), 0) & 7
    y_in = lax.broadcasted_iota(jnp.int32, (8 * levels, 8 * lev), 1) & 7
    wide_ref[...] = jnp.where(y_out == y_in, tall, 0.0).astype(jnp.bfloat16)
    stores = [pltpu.make_async_copy(wide_ref, wide_hbm, store.at[GROUPS])]
    stores[0].start()

    def lat_one(c, carry):
        own = lon[c]
        column = jnp.concatenate(
            [
                jnp.concatenate([north[c], own[: 2 * HALO]], axis=0),
                jnp.concatenate([own[TY - 2 * HALO :], south[c]], axis=0),
            ],
            axis=1,
        )
        got = jnp.dot(
            band[c, HALO : 2 * HALO, : 3 * HALO], column, preferred_element_type=jnp.float32
        ).astype(jnp.bfloat16)
        out_ref[c, :HALO] = got[:, :TX]
        out_ref[c, TY - HALO :] = got[:, TX:]
        return carry

    for g in range(GROUPS):

        @pl.when(has_up)
        def _(g=g):
            downs[g].wait_recv()

        @pl.when(has_down)
        def _(g=g):
            ups[g].wait_recv()

        lax.fori_loop(g * width, (g + 1) * width, lat_one, 0, unroll=4)
        chans = pl.ds(g * width, width)
        stores.append(pltpu.make_async_copy(out_ref.at[chans], out_hbm.at[chans], store.at[g]))
        stores[-1].start()

    for copy in stores:
        copy.wait()
    for copy in key_copies + over + [beside] + onward:
        copy.wait_send()
    for g in range(GROUPS):

        @pl.when(has_up)
        def _(g=g):
            ups[g].wait_send()

        @pl.when(has_down)
        def _(g=g):
            downs[g].wait_send()


def mix_kernel(wide_ref, field_ref, out_ref):
    levels = out_ref.shape[0]
    lev = field_ref.shape[0]
    field = field_ref[...].astype(jnp.float32)
    right = jnp.concatenate(
        [field[:, :8].reshape(8 * lev, TX), field[:, 8:].reshape(8 * lev, TX)], axis=1
    ).astype(jnp.bfloat16)
    got = jnp.dot(wide_ref[...], right, preferred_element_type=jnp.float32)
    out_ref[...] = jnp.concatenate(
        [got[:, :TX].reshape(levels, 8, TX), got[:, TX:].reshape(levels, 8, TX)], axis=1
    ).astype(jnp.bfloat16)


def gathered(innovation, owner_tile, cell_index, length_scale, eof_basis):
    n_lat = lax.axis_size("lat")
    lev, rec = innovation.shape
    levels = eof_basis.shape[0]
    hbm = pl.BlockSpec(memory_space=pltpu.HBM)
    smooth, wide = pl.pallas_call(
        functools.partial(smooth_kernel, n_lat),
        out_shape=(
            jax.ShapeDtypeStruct((lev, TY, TX), jnp.bfloat16),
            jax.ShapeDtypeStruct((8 * levels, 8 * lev), jnp.bfloat16),
        ),
        in_specs=[hbm] * 5,
        out_specs=(hbm, hbm),
        scratch_shapes=[
            pltpu.VMEM((lev, TY, TX), jnp.bfloat16),
            pltpu.VMEM((8 * levels, 8 * lev), jnp.bfloat16),
            pltpu.SemaphoreType.DMA((GROUPS + 1,)),
            pltpu.VMEM((lev, rec), jnp.bfloat16),
            pltpu.VMEM((1, rec), jnp.int32),
            pltpu.VMEM((rec,), jnp.int32),
            pltpu.VMEM((1, lev), jnp.float32),
            pltpu.VMEM((lev, levels), jnp.bfloat16),
            pltpu.SemaphoreType.DMA((5,)),
            pltpu.VMEM((1, rec), jnp.int32),
            pltpu.VMEM((3, lev, rec), jnp.bfloat16),
            pltpu.VMEM((3, 1, rec), jnp.int32),
            pltpu.VMEM((4, 8 * lev, rec), jnp.bfloat16),
            pltpu.VMEM((4, 5, 1, rec), jnp.float32),
            pltpu.VMEM((10, 8 * lev, TX), jnp.float32),
            pltpu.VMEM((lev, TX), jnp.float32),
            pltpu.VMEM((lev, 2 * TX, TX), jnp.bfloat16),
            pltpu.VMEM((lev, TY, TX), jnp.bfloat16),
            pltpu.VMEM((lev, HALO, TX), jnp.bfloat16),
            pltpu.VMEM((lev, HALO, TX), jnp.bfloat16),
            pltpu.SemaphoreType.DMA((5,)),
            pltpu.SemaphoreType.DMA((5,)),
            pltpu.SemaphoreType.DMA((3,)),
            pltpu.SemaphoreType.DMA((3,)),
            pltpu.SemaphoreType.DMA((2, GROUPS)),
            pltpu.SemaphoreType.DMA((2, GROUPS)),
        ],
        compiler_params=pltpu.CompilerParams(
            collective_id=0, has_side_effects=True, vmem_limit_bytes=58 * 1024 * 1024
        ),
        cost_estimate=pl.CostEstimate(
            flops=2 * 8 * lev * 4 * rec * 1280, bytes_accessed=8 * 1024 * 1024, transcendentals=0
        ),
    )(innovation, owner_tile.reshape(1, rec), cell_index, length_scale.reshape(1, lev), eof_basis.T)
    return pl.pallas_call(
        mix_kernel,
        out_shape=jax.ShapeDtypeStruct((levels, TY, TX), jnp.bfloat16),
        grid=(TY // 16,),
        in_specs=[
            pl.BlockSpec((8 * levels, 8 * lev), lambda g: (0, 0)),
            pl.BlockSpec((lev, 16, TX), lambda g: (0, g, 0)),
        ],
        out_specs=pl.BlockSpec((levels, 16, TX), lambda g: (0, g, 0)),
        compiler_params=pltpu.CompilerParams(vmem_limit_bytes=58 * 1024 * 1024),
    )(wide, smooth)


def solution(mesh):
    in_specs = (P(None, ("lon", "lat")), P(("lon", "lat"), None), P(("lon", "lat")), P(), P())
    out_specs = P(None, "lat", "lon")
    local = gathered if mesh.shape["lon"] == 4 else packed
    return jax.shard_map(local, mesh=mesh, in_specs=in_specs, out_specs=out_specs, check_vma=False)
```

```python
import functools

import jax
import jax.numpy as jnp
from jax import lax
from jax.experimental import pallas as pl
from jax.experimental.pallas import tpu as pltpu
from jax.sharding import PartitionSpec as P

TX = 128
TY = 64


def extended(shard, sides, width):
    for axis, dim in sides:
        size, length = (lax.axis_size(axis), shard.shape[dim])
        up = [(i, (i + 1) % size) for i in range(size)]
        down = [(j, i) for i, j in up]
        last = lax.slice_in_dim(shard, length - width, length, axis=dim)
        initial = lax.slice_in_dim(shard, 0, width, axis=dim)
        before = lax.ppermute(last, axis, up)
        after = lax.ppermute(initial, axis, down)
        shard = jnp.concatenate([before, shard, after], axis=dim)
    return shard


def tap_norm(scale):
    dist = jnp.arange(-15, 16).astype(jnp.float32)
    gauss = jnp.exp(-(dist[None, :] * dist[None, :]) / (2.0 * scale[:, None] * scale[:, None]))
    return jnp.sqrt(jnp.sum(gauss * gauss, axis=1))


def tap_weight(dist, scale, norm):
    value = jnp.exp(-(dist * dist) / (2.0 * scale * scale)) / norm
    return jnp.where(jnp.abs(dist) <= 15.0, value, 0.0)


def band_matrix(scale, norm, inner, outer, offset):
    inner_pos = jnp.arange(inner).astype(jnp.float32)[:, None]
    outer_pos = jnp.arange(outer).astype(jnp.float32)[None, :]
    dist = inner_pos - offset - outer_pos
    return tap_weight(dist[None], scale[:, None, None], norm[:, None, None]).astype(jnp.bfloat16)


def slot_numbers(dest, keep, n_lon):
    hits = ((dest[:, None] == jnp.arange(n_lon, dtype=jnp.int32)[None, :]) & keep[:, None]).astype(
        jnp.int32
    )
    before = jnp.cumsum(hits, axis=0) - hits
    return jnp.sum(before * hits, axis=1)


def spread_block(part, where, width):
    cells = jnp.arange(TY * width, dtype=jnp.int32)
    grid_row = (cells // width).astype(jnp.bfloat16)
    grid_col = (cells % width).astype(jnp.bfloat16)
    onehot = (
        (where[0][:, None] == grid_row[None, :]) & (where[1][:, None] == grid_col[None, :])
    ).astype(jnp.bfloat16)
    return jnp.dot(part, onehot, preferred_element_type=jnp.float32)


def packed(innovation, owner_tile, cell_index, length_scale, eof_basis):
    n_lon = lax.axis_size("lon")
    lev, rec = innovation.shape
    cap = (2 * rec + n_lon - 1) // n_lon
    owner = owner_tile[:, 0]
    cell_row = cell_index // TX
    cell_col = cell_index % TX
    everyone = jnp.ones((rec,), jnp.bool_)
    target = owner * cap + slot_numbers(owner, everyone, n_lon)
    values = jnp.zeros((lev, n_lon * cap), jnp.bfloat16).at[:, target].set(innovation)
    coords = jnp.stack([cell_row, cell_col]).astype(jnp.bfloat16)
    places = jnp.full((2, n_lon * cap), -1.0, jnp.bfloat16).at[:, target].set(coords)
    values = values.reshape(lev, n_lon, cap)
    places = places.reshape(2, n_lon, cap)
    got_values, got_places = (
        lax.all_to_all(values, "lon", split_axis=1, concat_axis=1, tiled=True),
        lax.all_to_all(places, "lon", split_axis=1, concat_axis=1, tiled=True),
    )

    def spread_one(source, total):
        part = lax.dynamic_index_in_dim(got_values, source, 1, keepdims=False)
        where = lax.dynamic_index_in_dim(got_places, source, 1, keepdims=False)
        return total + spread_block(part, where, TX)

    summed = lax.fori_loop(0, n_lon, spread_one, jnp.zeros((lev, TY * TX), jnp.float32))
    spread = summed.astype(jnp.bfloat16).reshape(lev, TY, TX)
    padded = extended(spread, (("lon", 2),), 15)
    norm = tap_norm(length_scale)
    band_lon = band_matrix(length_scale, norm, TX + 30, TX, 15.0)
    lon_smooth = jnp.einsum(
        "cyk,ckx->cyx", padded, band_lon, preferred_element_type=jnp.float32
    ).astype(jnp.bfloat16)
    n_lat = lax.axis_size("lat")
    south = [(i, i + 1) for i in range(n_lat - 1)]
    north = [(j, i) for i, j in south]
    above = lax.ppermute(lon_smooth[:, TY - 16 :], "lat", south)
    below = lax.ppermute(lon_smooth[:, :16], "lat", north)
    column = jnp.concatenate([above, lon_smooth, below], axis=1)
    band_lat = band_matrix(length_scale, norm, TY + 32, TY, 16.0)
    smooth = jnp.einsum(
        "cky,ckx->cyx", band_lat, column, preferred_element_type=jnp.float32
    ).astype(jnp.bfloat16)
    return jnp.einsum("lc,cyx->lyx", eof_basis, smooth, preferred_element_type=jnp.float32).astype(
        jnp.bfloat16
    )


MESH = pl.DeviceIdType.MESH
HALO = 16
GROUPS = 4


def copies(ref_from, ref_to, send, recv, target):
    return pltpu.make_async_remote_copy(
        src_ref=ref_from,
        dst_ref=ref_to,
        send_sem=send,
        recv_sem=recv,
        device_id=target,
        device_id_type=MESH,
    )


def smooth_kernel(
    n_lat, innov_hbm, owner_hbm, cell_hbm, scale_hbm, eof_hbm, out_hbm, wide_hbm,
    out_ref, wide_ref, store,
    innov_ref, owner_ref, cell_ref, scale_ref, eof_ref, load, key_ref, vals, keys, picked, slots, sums, weights, band, lon, north, south,
    val_send, val_recv, key_send, key_recv, halo_send, halo_recv,
):
    lev, rec = innov_ref.shape
    levels = eof_ref.shape[1]
    loads = [
        pltpu.make_async_copy(there, here, load.at[i])
        for i, (there, here) in enumerate(
            (
                (owner_hbm, owner_ref),
                (cell_hbm, cell_ref),
                (innov_hbm, innov_ref),
                (scale_hbm, scale_ref),
                (eof_hbm, eof_ref),
            )
        )
    ]
    for copy in loads:
        copy.start()
    half = rec // 2
    me = lax.axis_index("lon")
    lat = lax.axis_index("lat")
    partner = me + 1 - 2 * (me % 2)
    across = (me + 2) % 4
    far = (partner + 2) % 4
    has_up = lat > 0
    has_down = lat < n_lat - 1

    barrier = pltpu.get_barrier_semaphore()
    for peer in (partner, across, far):
        pl.semaphore_signal(barrier, inc=1, device_id=(peer, lat), device_id_type=MESH)

    @pl.when(has_up)
    def _():
        pl.semaphore_signal(barrier, inc=1, device_id=(me, lat - 1), device_id_type=MESH)

    @pl.when(has_down)
    def _():
        pl.semaphore_signal(barrier, inc=1, device_id=(me, lat + 1), device_id_type=MESH)

    loads[0].wait()
    loads[1].wait()
    cell = cell_ref[...].reshape(1, rec)
    key_ref[...] = (cell >> 7) * 512 + owner_ref[...] * TX + (cell & (TX - 1))
    pl.semaphore_wait(barrier, 3 + has_up.astype(jnp.int32) + has_down.astype(jnp.int32))

    key_copies = [
        copies(key_ref, keys.at[i], key_send.at[i], key_recv.at[i], (peer, lat))
        for i, peer in enumerate((partner, across, far))
    ]
    parts = [pl.ds(0, half), pl.ds(half, half)]
    over = [
        copies(
            innov_hbm.at[:, parts[h]], vals.at[1, :, parts[h]],
            val_send.at[h], val_recv.at[h], (across, lat),
        )
        for h in range(2)
    ]
    beside = copies(innov_hbm, vals.at[0], val_send.at[2], val_recv.at[2], (partner, lat))
    onward = [
        copies(
            vals.at[1, :, parts[h]], vals.at[2, :, parts[h]],
            val_send.at[3 + h], val_recv.at[3 + h], (partner, lat),
        )
        for h in range(2)
    ]
    for copy in key_copies:
        copy.start()
    over[0].start()
    over[1].start()
    beside.start()

    row_of = lax.broadcasted_iota(jnp.int32, (256, rec), 0).astype(jnp.float32).astype(jnp.bfloat16)
    zero = jnp.zeros((), jnp.bfloat16)
    one = jnp.ones((), jnp.bfloat16)

    def sort_out(part, key, at):
        row = key >> 9
        rel = ((key & 511) - TX * me + HALO) & 511
        sub = (row & 7).astype(jnp.float32).astype(jnp.bfloat16)
        phase = row >> 3
        inside = (rel >= HALO) & (rel < HALO + TX)
        main = (phase & 1) * TX + rel - HALO
        for n, pair in ((0, 0), (1, 3), (3, 1), (4, 2)):
            hit = inside & ((phase >> 1) == pair)
            slots[at, n] = jnp.where(hit, main, -1).astype(jnp.float32)
        rim = jnp.where(rel < HALO, rel, rel - TX)
        rim_hit = (rel < HALO) | ((rel >= HALO + TX) & (rel < 2 * HALO + TX))
        slots[at, 2] = jnp.where(rim_hit, phase * 2 * HALO + rim, -1).astype(jnp.float32)
        values = part[...]
        for t in range(8):
            mine = sub == jnp.full((), t, jnp.bfloat16)
            picked[at, pl.ds(t * lev, lev), :] = jnp.where(mine, values, zero)

    def spread(blocks, tiles, first=False):
        def tile(n, carry):
            got = None
            for at in blocks:
                where = slots[at, n].astype(jnp.bfloat16)
                onehot = jnp.where(row_of == where, one, zero)
                term = lax.dot_general(
                    picked[at], onehot, (((1,), (1,)), ((), ())),
                    preferred_element_type=jnp.float32,
                )
                got = term if got is None else got + term
            for side in range(2):
                piece = got[:, side * TX : (side + 1) * TX]
                if first:
                    sums[2 * n + side] = piece
                else:
                    sums[2 * n + side] += piece
            return carry

        lax.fori_loop(tiles[0], tiles[1], tile, 0)

    loads[2].wait()
    sort_out(innov_ref, key_ref[...], 0)
    spread([0], (0, 3), True)

    line = lax.broadcasted_iota(jnp.int32, (lev, TX), 1)
    near = jnp.where(line < TX // 2, line, line - TX).astype(jnp.float32)
    loads[3].wait()
    diagonal = lax.broadcasted_iota(jnp.int32, (lev, lev), 0) == lax.broadcasted_iota(
        jnp.int32, (lev, lev), 1
    )
    scale = jnp.sum(
        jnp.where(diagonal, jnp.broadcast_to(scale_ref[...], (lev, lev)), 0.0), axis=1, keepdims=True
    )
    gauss = jnp.where(
        jnp.abs(near) <= 15.0, jnp.exp(-(near * near) / (2.0 * scale * scale)), 0.0
    )
    norm = jnp.sqrt(jnp.sum(gauss * gauss, axis=1, keepdims=True))
    weights[...] = gauss / norm
    west = lax.broadcasted_iota(jnp.int32, (HALO, TX), 1) < TX // 2

    def band_one(c, carry):
        start = pltpu.roll(
            jnp.broadcast_to(weights[pl.ds(c, 1), :], (8, TX)), 0, 1, stride=1, stride_axis=0
        )
        turned = [start] + [pltpu.roll(start, 8 * i, 1) for i in range(1, TX // 8)]
        top = jnp.concatenate(turned[:2], axis=0)
        bottom = jnp.concatenate(turned[-2:], axis=0)
        band[c, :HALO] = jnp.where(west, top, 0.0).astype(jnp.bfloat16)
        band[c, HALO : TX - HALO] = jnp.concatenate(turned[2:-2], axis=0).astype(jnp.bfloat16)
        band[c, TX - HALO : TX] = jnp.where(west, 0.0, bottom).astype(jnp.bfloat16)
        rim = jnp.concatenate(
            [jnp.where(west, bottom, 0.0), jnp.where(west, 0.0, top)], axis=0
        ).astype(jnp.bfloat16)
        for t in range(4):
            band[c, TX + 2 * HALO * t : TX + 2 * HALO * (t + 1)] = rim
        return carry

    lax.fori_loop(0, lev, band_one, 0, unroll=4)

    key_copies[0].wait_recv()
    beside.wait_recv()
    sort_out(vals.at[0], keys[0], 1)
    spread([1], (0, 3))
    for h in range(2):
        over[h].wait_recv()
        onward[h].start()
    key_copies[1].wait_recv()
    sort_out(vals.at[1], keys[1], 2)
    spread([2], (0, 3))
    key_copies[2].wait_recv()
    for h in range(2):
        onward[h].wait_recv()
    sort_out(vals.at[2], keys[2], 3)
    spread([3], (0, 3))

    lane = lax.broadcasted_iota(jnp.int32, (8, TX), 1) >> 5
    width = lev // GROUPS
    spot = (0, 1, 6, 7, 8, 9, 2, 3)

    def lon_rows(c, phases):
        rows = pl.ds(c, 8, stride=lev)
        main = [sums[spot[p], rows, :] for p in phases]
        rim = [jnp.where(lane == p % 4, sums[4 + p // 4, rows, :], 0.0) for p in phases]
        left = jnp.concatenate(
            [jnp.concatenate(main, axis=0), jnp.concatenate(rim, axis=0)], axis=1
        ).astype(jnp.bfloat16)
        return jnp.dot(left, band[c], preferred_element_type=jnp.float32).astype(jnp.bfloat16)

    def lon_one(c, carry):
        got = lon_rows(c, (0, 1, 6, 7))
        lon[c, :HALO] = got[:HALO]
        lon[c, TY - HALO :] = got[HALO:]
        return carry

    def mid_one(c, carry):
        lon[c, HALO : TY - HALO] = lon_rows(c, (2, 3, 4, 5))
        return carry

    def inner_one(c, carry):
        out_ref[c, HALO : TY - HALO] = jnp.dot(
            band[c, HALO : TY - HALO, :TY], lon[c], preferred_element_type=jnp.float32
        ).astype(jnp.bfloat16)
        return carry

    ups, downs = [], []
    for g in range(GROUPS):
        lax.fori_loop(g * width, (g + 1) * width, lon_one, 0, unroll=4)
        chans = pl.ds(g * width, width)
        up = copies(
            lon.at[chans, pl.ds(0, HALO), :], south.at[chans],
            halo_send.at[0, g], halo_recv.at[0, g], (me, lat - 1),
        )
        down = copies(
            lon.at[chans, pl.ds(TY - HALO, HALO), :], north.at[chans],
            halo_send.at[1, g], halo_recv.at[1, g], (me, lat + 1),
        )
        ups.append(up)
        downs.append(down)

        @pl.when(has_up)
        def _(up=up):
            up.start()

        @pl.when(has_down)
        def _(down=down):
            down.start()

    @pl.when(jnp.logical_not(has_up))
    def _():
        north[...] = jnp.zeros_like(north)

    @pl.when(jnp.logical_not(has_down))
    def _():
        south[...] = jnp.zeros_like(south)

    spread([0, 1, 2, 3], (3, 5), True)
    lax.fori_loop(0, lev, mid_one, 0, unroll=4)
    lax.fori_loop(0, lev, inner_one, 0, unroll=4)

    loads[4].wait()
    copy_of = lax.broadcasted_iota(jnp.int32, (lev, 8 * lev), 1) >> 3
    chan = lax.broadcasted_iota(jnp.int32, (lev, 8 * lev), 0)
    repeat = jnp.where(copy_of == chan, 1.0, 0.0).astype(jnp.bfloat16)
    flat = lax.dot_general(
        eof_ref[...], repeat, (((0,), (0,)), ((), ())), preferred_element_type=jnp.float32
    ).astype(jnp.bfloat16)
    row = lax.broadcasted_iota(jnp.int32, (8 * levels, levels), 0) >> 3
    level = lax.broadcasted_iota(jnp.int32, (8 * levels, levels), 1)
    down_all = jnp.where(row == level, 1.0, 0.0).astype(jnp.bfloat16)
    tall = jnp.dot(down_all, flat, preferred_element_type=jnp.float32)
    y_out = lax.broadcasted_iota(jnp.int32, (8 * levels, 8 * lev), 0) & 7
    y_in = lax.broadcasted_iota(jnp.int32, (8 * levels, 8 * lev), 1) & 7
    wide_ref[...] = jnp.where(y_out == y_in, tall, 0.0).astype(jnp.bfloat16)
    stores = [pltpu.make_async_copy(wide_ref, wide_hbm, store.at[GROUPS])]
    stores[0].start()

    def lat_one(c, carry):
        own = lon[c]
        column = jnp.concatenate(
            [
                jnp.concatenate([north[c], own[: 2 * HALO]], axis=0),
                jnp.concatenate([own[TY - 2 * HALO :], south[c]], axis=0),
            ],
            axis=1,
        )
        got = jnp.dot(
            band[c, HALO : 2 * HALO, : 3 * HALO], column, preferred_element_type=jnp.float32
        ).astype(jnp.bfloat16)
        out_ref[c, :HALO] = got[:, :TX]
        out_ref[c, TY - HALO :] = got[:, TX:]
        return carry

    for g in range(GROUPS):

        @pl.when(has_up)
        def _(g=g):
            downs[g].wait_recv()

        @pl.when(has_down)
        def _(g=g):
            ups[g].wait_recv()

        lax.fori_loop(g * width, (g + 1) * width, lat_one, 0, unroll=4)
        chans = pl.ds(g * width, width)
        stores.append(pltpu.make_async_copy(out_ref.at[chans], out_hbm.at[chans], store.at[g]))
        stores[-1].start()

    for copy in stores:
        copy.wait()
    for copy in key_copies + over + [beside] + onward:
        copy.wait_send()
    for g in range(GROUPS):

        @pl.when(has_up)
        def _(g=g):
            ups[g].wait_send()

        @pl.when(has_down)
        def _(g=g):
            downs[g].wait_send()


def mix_kernel(wide_hbm, field_hbm, out_hbm, wide, fields, outs, sems):
    parts, lev = fields.shape[:2]
    levels = outs.shape[1]
    bands = [pl.ds(16 * g, 16) for g in range(parts)]
    first = pltpu.make_async_copy(wide_hbm, wide, sems.at[0])
    loads = [
        pltpu.make_async_copy(field_hbm.at[:, bands[g], :], fields.at[g], sems.at[1 + g])
        for g in range(parts)
    ]
    stores = [
        pltpu.make_async_copy(outs.at[g], out_hbm.at[:, bands[g], :], sems.at[1 + parts + g])
        for g in range(parts)
    ]
    first.start()
    for load in loads:
        load.start()
    first.wait()
    for g in range(parts):
        loads[g].wait()
        field = fields[g].astype(jnp.float32)
        right = jnp.concatenate(
            [field[:, :8].reshape(8 * lev, TX), field[:, 8:].reshape(8 * lev, TX)], axis=1
        ).astype(jnp.bfloat16)
        got = jnp.dot(wide[...], right, preferred_element_type=jnp.float32)
        outs[g] = jnp.concatenate(
            [got[:, :TX].reshape(levels, 8, TX), got[:, TX:].reshape(levels, 8, TX)], axis=1
        ).astype(jnp.bfloat16)
        stores[g].start()
    for store in stores:
        store.wait()


def gathered(innovation, owner_tile, cell_index, length_scale, eof_basis):
    n_lat = lax.axis_size("lat")
    lev, rec = innovation.shape
    levels = eof_basis.shape[0]
    hbm = pl.BlockSpec(memory_space=pltpu.HBM)
    smooth, wide = pl.pallas_call(
        functools.partial(smooth_kernel, n_lat),
        out_shape=(
            jax.ShapeDtypeStruct((lev, TY, TX), jnp.bfloat16),
            jax.ShapeDtypeStruct((8 * levels, 8 * lev), jnp.bfloat16),
        ),
        in_specs=[hbm] * 5,
        out_specs=(hbm, hbm),
        scratch_shapes=[
            pltpu.VMEM((lev, TY, TX), jnp.bfloat16),
            pltpu.VMEM((8 * levels, 8 * lev), jnp.bfloat16),
            pltpu.SemaphoreType.DMA((GROUPS + 1,)),
            pltpu.VMEM((lev, rec), jnp.bfloat16),
            pltpu.VMEM((1, rec), jnp.int32),
            pltpu.VMEM((rec,), jnp.int32),
            pltpu.VMEM((1, lev), jnp.float32),
            pltpu.VMEM((lev, levels), jnp.bfloat16),
            pltpu.SemaphoreType.DMA((5,)),
            pltpu.VMEM((1, rec), jnp.int32),
            pltpu.VMEM((3, lev, rec), jnp.bfloat16),
            pltpu.VMEM((3, 1, rec), jnp.int32),
            pltpu.VMEM((4, 8 * lev, rec), jnp.bfloat16),
            pltpu.VMEM((4, 5, 1, rec), jnp.float32),
            pltpu.VMEM((10, 8 * lev, TX), jnp.float32),
            pltpu.VMEM((lev, TX), jnp.float32),
            pltpu.VMEM((lev, 2 * TX, TX), jnp.bfloat16),
            pltpu.VMEM((lev, TY, TX), jnp.bfloat16),
            pltpu.VMEM((lev, HALO, TX), jnp.bfloat16),
            pltpu.VMEM((lev, HALO, TX), jnp.bfloat16),
            pltpu.SemaphoreType.DMA((5,)),
            pltpu.SemaphoreType.DMA((5,)),
            pltpu.SemaphoreType.DMA((3,)),
            pltpu.SemaphoreType.DMA((3,)),
            pltpu.SemaphoreType.DMA((2, GROUPS)),
            pltpu.SemaphoreType.DMA((2, GROUPS)),
        ],
        compiler_params=pltpu.CompilerParams(
            collective_id=0, has_side_effects=True, vmem_limit_bytes=58 * 1024 * 1024
        ),
        cost_estimate=pl.CostEstimate(
            flops=2 * 8 * lev * 4 * rec * 1280, bytes_accessed=8 * 1024 * 1024, transcendentals=0
        ),
    )(innovation, owner_tile.reshape(1, rec), cell_index, length_scale.reshape(1, lev), eof_basis.T)
    return pl.pallas_call(
        mix_kernel,
        out_shape=jax.ShapeDtypeStruct((levels, TY, TX), jnp.bfloat16),
        in_specs=[hbm, hbm],
        out_specs=hbm,
        scratch_shapes=[
            pltpu.VMEM((8 * levels, 8 * lev), jnp.bfloat16),
            pltpu.VMEM((TY // 16, lev, 16, TX), jnp.bfloat16),
            pltpu.VMEM((TY // 16, levels, 16, TX), jnp.bfloat16),
            pltpu.SemaphoreType.DMA((1 + 2 * (TY // 16),)),
        ],
        compiler_params=pltpu.CompilerParams(vmem_limit_bytes=58 * 1024 * 1024),
    )(wide, smooth)


def solution(mesh):
    in_specs = (P(None, ("lon", "lat")), P(("lon", "lat"), None), P(("lon", "lat")), P(), P())
    out_specs = P(None, "lat", "lon")
    local = gathered if mesh.shape["lon"] == 4 else packed
    return jax.shard_map(local, mesh=mesh, in_specs=in_specs, out_specs=out_specs, check_vma=False)
```

```python
import functools

import jax
import jax.numpy as jnp
from jax import lax
from jax.experimental import pallas as pl
from jax.experimental.pallas import tpu as pltpu
from jax.sharding import PartitionSpec as P

TX = 128
TY = 64


def extended(shard, sides, width):
    for axis, dim in sides:
        size, length = (lax.axis_size(axis), shard.shape[dim])
        up = [(i, (i + 1) % size) for i in range(size)]
        down = [(j, i) for i, j in up]
        last = lax.slice_in_dim(shard, length - width, length, axis=dim)
        initial = lax.slice_in_dim(shard, 0, width, axis=dim)
        before = lax.ppermute(last, axis, up)
        after = lax.ppermute(initial, axis, down)
        shard = jnp.concatenate([before, shard, after], axis=dim)
    return shard


def tap_norm(scale):
    dist = jnp.arange(-15, 16).astype(jnp.float32)
    gauss = jnp.exp(-(dist[None, :] * dist[None, :]) / (2.0 * scale[:, None] * scale[:, None]))
    return jnp.sqrt(jnp.sum(gauss * gauss, axis=1))


def tap_weight(dist, scale, norm):
    value = jnp.exp(-(dist * dist) / (2.0 * scale * scale)) / norm
    return jnp.where(jnp.abs(dist) <= 15.0, value, 0.0)


def band_matrix(scale, norm, inner, outer, offset):
    inner_pos = jnp.arange(inner).astype(jnp.float32)[:, None]
    outer_pos = jnp.arange(outer).astype(jnp.float32)[None, :]
    dist = inner_pos - offset - outer_pos
    return tap_weight(dist[None], scale[:, None, None], norm[:, None, None]).astype(jnp.bfloat16)


def slot_numbers(dest, keep, n_lon):
    hits = ((dest[:, None] == jnp.arange(n_lon, dtype=jnp.int32)[None, :]) & keep[:, None]).astype(
        jnp.int32
    )
    before = jnp.cumsum(hits, axis=0) - hits
    return jnp.sum(before * hits, axis=1)


def spread_block(part, where, width):
    cells = jnp.arange(TY * width, dtype=jnp.int32)
    grid_row = (cells // width).astype(jnp.bfloat16)
    grid_col = (cells % width).astype(jnp.bfloat16)
    onehot = (
        (where[0][:, None] == grid_row[None, :]) & (where[1][:, None] == grid_col[None, :])
    ).astype(jnp.bfloat16)
    return jnp.dot(part, onehot, preferred_element_type=jnp.float32)


def packed(innovation, owner_tile, cell_index, length_scale, eof_basis):
    n_lon = lax.axis_size("lon")
    lev, rec = innovation.shape
    cap = (2 * rec + n_lon - 1) // n_lon
    owner = owner_tile[:, 0]
    cell_row = cell_index // TX
    cell_col = cell_index % TX
    everyone = jnp.ones((rec,), jnp.bool_)
    target = owner * cap + slot_numbers(owner, everyone, n_lon)
    values = jnp.zeros((lev, n_lon * cap), jnp.bfloat16).at[:, target].set(innovation)
    coords = jnp.stack([cell_row, cell_col]).astype(jnp.bfloat16)
    places = jnp.full((2, n_lon * cap), -1.0, jnp.bfloat16).at[:, target].set(coords)
    values = values.reshape(lev, n_lon, cap)
    places = places.reshape(2, n_lon, cap)
    got_values, got_places = (
        lax.all_to_all(values, "lon", split_axis=1, concat_axis=1, tiled=True),
        lax.all_to_all(places, "lon", split_axis=1, concat_axis=1, tiled=True),
    )

    def spread_one(source, total):
        part = lax.dynamic_index_in_dim(got_values, source, 1, keepdims=False)
        where = lax.dynamic_index_in_dim(got_places, source, 1, keepdims=False)
        return total + spread_block(part, where, TX)

    summed = lax.fori_loop(0, n_lon, spread_one, jnp.zeros((lev, TY * TX), jnp.float32))
    spread = summed.astype(jnp.bfloat16).reshape(lev, TY, TX)
    padded = extended(spread, (("lon", 2),), 15)
    norm = tap_norm(length_scale)
    band_lon = band_matrix(length_scale, norm, TX + 30, TX, 15.0)
    lon_smooth = jnp.einsum(
        "cyk,ckx->cyx", padded, band_lon, preferred_element_type=jnp.float32
    ).astype(jnp.bfloat16)
    n_lat = lax.axis_size("lat")
    south = [(i, i + 1) for i in range(n_lat - 1)]
    north = [(j, i) for i, j in south]
    above = lax.ppermute(lon_smooth[:, TY - 16 :], "lat", south)
    below = lax.ppermute(lon_smooth[:, :16], "lat", north)
    column = jnp.concatenate([above, lon_smooth, below], axis=1)
    band_lat = band_matrix(length_scale, norm, TY + 32, TY, 16.0)
    smooth = jnp.einsum(
        "cky,ckx->cyx", band_lat, column, preferred_element_type=jnp.float32
    ).astype(jnp.bfloat16)
    return jnp.einsum("lc,cyx->lyx", eof_basis, smooth, preferred_element_type=jnp.float32).astype(
        jnp.bfloat16
    )


MESH = pl.DeviceIdType.MESH
HALO = 16
GROUPS = 4


def copies(ref_from, ref_to, send, recv, target):
    return pltpu.make_async_remote_copy(
        src_ref=ref_from,
        dst_ref=ref_to,
        send_sem=send,
        recv_sem=recv,
        device_id=target,
        device_id_type=MESH,
    )


def smooth_kernel(
    n_lat, innov_hbm, owner_hbm, cell_hbm, scale_hbm, eof_hbm, out_hbm, wide_hbm,
    out_ref, wide_ref, store,
    innov_ref, owner_ref, cell_ref, scale_ref, eof_ref, load, key_ref, vals, keys, picked, slots, sums, weights, band, lon, north, south,
    val_send, val_recv, key_send, key_recv, halo_send, halo_recv,
):
    lev, rec = innov_ref.shape
    levels = eof_ref.shape[1]
    loads = [
        pltpu.make_async_copy(there, here, load.at[i])
        for i, (there, here) in enumerate(
            (
                (owner_hbm, owner_ref),
                (cell_hbm, cell_ref),
                (innov_hbm, innov_ref),
                (scale_hbm, scale_ref),
                (eof_hbm, eof_ref),
            )
        )
    ]
    for copy in loads:
        copy.start()
    half = rec // 2
    me = lax.axis_index("lon")
    lat = lax.axis_index("lat")
    partner = me + 1 - 2 * (me % 2)
    across = (me + 2) % 4
    far = (partner + 2) % 4
    has_up = lat > 0
    has_down = lat < n_lat - 1

    barrier = pltpu.get_barrier_semaphore()
    for peer in (partner, across, far):
        pl.semaphore_signal(barrier, inc=1, device_id=(peer, lat), device_id_type=MESH)

    @pl.when(has_up)
    def _():
        pl.semaphore_signal(barrier, inc=1, device_id=(me, lat - 1), device_id_type=MESH)

    @pl.when(has_down)
    def _():
        pl.semaphore_signal(barrier, inc=1, device_id=(me, lat + 1), device_id_type=MESH)

    loads[0].wait()
    loads[1].wait()
    cell = cell_ref[...].reshape(1, rec)
    key_ref[...] = (cell >> 7) * 512 + owner_ref[...] * TX + (cell & (TX - 1))
    pl.semaphore_wait(barrier, 3 + has_up.astype(jnp.int32) + has_down.astype(jnp.int32))

    key_copies = [
        copies(key_ref, keys.at[i], key_send.at[i], key_recv.at[i], (peer, lat))
        for i, peer in enumerate((partner, across, far))
    ]
    parts = [pl.ds(0, half), pl.ds(half, half)]
    over = [
        copies(
            innov_hbm.at[:, parts[h]], vals.at[1, :, parts[h]],
            val_send.at[h], val_recv.at[h], (across, lat),
        )
        for h in range(2)
    ]
    beside = copies(innov_hbm, vals.at[0], val_send.at[2], val_recv.at[2], (partner, lat))
    onward = [
        copies(
            vals.at[1, :, parts[h]], vals.at[2, :, parts[h]],
            val_send.at[3 + h], val_recv.at[3 + h], (partner, lat),
        )
        for h in range(2)
    ]
    for copy in key_copies:
        copy.start()
    over[0].start()
    over[1].start()
    beside.start()

    row_of = lax.broadcasted_iota(jnp.int32, (256, rec), 0).astype(jnp.float32).astype(jnp.bfloat16)
    zero = jnp.zeros((), jnp.bfloat16)
    one = jnp.ones((), jnp.bfloat16)

    def sort_out(part, key, at):
        row = key >> 9
        rel = ((key & 511) - TX * me + HALO) & 511
        sub = (row & 7).astype(jnp.float32).astype(jnp.bfloat16)
        phase = row >> 3
        inside = (rel >= HALO) & (rel < HALO + TX)
        main = (phase & 1) * TX + rel - HALO
        for n, pair in ((0, 0), (1, 3), (3, 1), (4, 2)):
            hit = inside & ((phase >> 1) == pair)
            slots[at, n] = jnp.where(hit, main, -1).astype(jnp.float32)
        rim = jnp.where(rel < HALO, rel, rel - TX)
        rim_hit = (rel < HALO) | ((rel >= HALO + TX) & (rel < 2 * HALO + TX))
        slots[at, 2] = jnp.where(rim_hit, phase * 2 * HALO + rim, -1).astype(jnp.float32)
        values = part[...]
        for t in range(8):
            mine = sub == jnp.full((), t, jnp.bfloat16)
            picked[at, pl.ds(t * lev, lev), :] = jnp.where(mine, values, zero)

    def spread(blocks, tiles, first=False):
        got = None
        for at in blocks:
            onehot = jnp.concatenate(
                [
                    jnp.where(row_of == slots[at, n].astype(jnp.bfloat16), one, zero)
                    for n in range(*tiles)
                ],
                axis=0,
            )
            term = lax.dot_general(
                picked[at], onehot, (((1,), (1,)), ((), ())), preferred_element_type=jnp.float32
            )
            got = term if got is None else got + term
        for i in range(2 * (tiles[1] - tiles[0])):
            piece = got[:, i * TX : (i + 1) * TX]
            if first:
                sums[2 * tiles[0] + i] = piece
            else:
                sums[2 * tiles[0] + i] += piece

    loads[2].wait()
    sort_out(innov_ref, key_ref[...], 0)
    spread([0], (0, 3), True)

    line = lax.broadcasted_iota(jnp.int32, (lev, TX), 1)
    near = jnp.where(line < TX // 2, line, line - TX).astype(jnp.float32)
    loads[3].wait()
    diagonal = lax.broadcasted_iota(jnp.int32, (lev, lev), 0) == lax.broadcasted_iota(
        jnp.int32, (lev, lev), 1
    )
    scale = jnp.sum(
        jnp.where(diagonal, jnp.broadcast_to(scale_ref[...], (lev, lev)), 0.0), axis=1, keepdims=True
    )
    gauss = jnp.where(
        jnp.abs(near) <= 15.0, jnp.exp(-(near * near) / (2.0 * scale * scale)), 0.0
    )
    norm = jnp.sqrt(jnp.sum(gauss * gauss, axis=1, keepdims=True))
    weights[...] = gauss / norm
    down_at = lax.broadcasted_iota(jnp.int32, (TX, TX), 0)
    side_at = lax.broadcasted_iota(jnp.int32, (TX, TX), 1)
    straight = jnp.abs(down_at - side_at) < TX // 2
    west = side_at[:HALO] < TX // 2

    def band_one(c, carry):
        ring = pltpu.roll(
            jnp.broadcast_to(weights[pl.ds(c, 1), :], (TX, TX)), 0, 1, stride=1, stride_axis=0
        )
        band[c, :TX] = jnp.where(straight, ring, 0.0).astype(jnp.bfloat16)
        rim = jnp.concatenate(
            [jnp.where(west, ring[TX - HALO :], 0.0), jnp.where(west, 0.0, ring[:HALO])], axis=0
        ).astype(jnp.bfloat16)
        for t in range(4):
            band[c, TX + 2 * HALO * t : TX + 2 * HALO * (t + 1)] = rim
        return carry

    lax.fori_loop(0, lev, band_one, 0, unroll=4)

    key_copies[0].wait_recv()
    beside.wait_recv()
    sort_out(vals.at[0], keys[0], 1)
    spread([1], (0, 3))
    for h in range(2):
        over[h].wait_recv()
        onward[h].start()
    key_copies[1].wait_recv()
    sort_out(vals.at[1], keys[1], 2)
    spread([2], (0, 3))
    key_copies[2].wait_recv()
    for h in range(2):
        onward[h].wait_recv()
    sort_out(vals.at[2], keys[2], 3)
    spread([3], (0, 3))

    lane = lax.broadcasted_iota(jnp.int32, (8, TX), 1) >> 5
    width = lev // GROUPS
    spot = (0, 1, 6, 7, 8, 9, 2, 3)

    def lon_rows(c, phases):
        rows = pl.ds(c, 8, stride=lev)
        main = [sums[spot[p], rows, :] for p in phases]
        rim = [jnp.where(lane == p % 4, sums[4 + p // 4, rows, :], 0.0) for p in phases]
        left = jnp.concatenate(
            [jnp.concatenate(main, axis=0), jnp.concatenate(rim, axis=0)], axis=1
        ).astype(jnp.bfloat16)
        return jnp.dot(left, band[c], preferred_element_type=jnp.float32).astype(jnp.bfloat16)

    def lon_one(c, carry):
        got = lon_rows(c, (0, 1, 6, 7))
        lon[c, :HALO] = got[:HALO]
        lon[c, TY - HALO :] = got[HALO:]
        return carry

    def mid_one(c, carry):
        lon[c, HALO : TY - HALO] = lon_rows(c, (2, 3, 4, 5))
        return carry

    def inner_one(c, carry):
        out_ref[c, HALO : TY - HALO] = jnp.dot(
            band[c, HALO : TY - HALO, :TY], lon[c], preferred_element_type=jnp.float32
        ).astype(jnp.bfloat16)
        return carry

    ups, downs = [], []
    for g in range(GROUPS):
        lax.fori_loop(g * width, (g + 1) * width, lon_one, 0, unroll=4)
        chans = pl.ds(g * width, width)
        up = copies(
            lon.at[chans, pl.ds(0, HALO), :], south.at[chans],
            halo_send.at[0, g], halo_recv.at[0, g], (me, lat - 1),
        )
        down = copies(
            lon.at[chans, pl.ds(TY - HALO, HALO), :], north.at[chans],
            halo_send.at[1, g], halo_recv.at[1, g], (me, lat + 1),
        )
        ups.append(up)
        downs.append(down)

        @pl.when(has_up)
        def _(up=up):
            up.start()

        @pl.when(has_down)
        def _(down=down):
            down.start()

    @pl.when(jnp.logical_not(has_up))
    def _():
        north[...] = jnp.zeros_like(north)

    @pl.when(jnp.logical_not(has_down))
    def _():
        south[...] = jnp.zeros_like(south)

    spread([0, 1, 2, 3], (3, 5), True)
    lax.fori_loop(0, lev, mid_one, 0, unroll=4)
    lax.fori_loop(0, lev, inner_one, 0, unroll=4)

    loads[4].wait()
    copy_of = lax.broadcasted_iota(jnp.int32, (lev, 8 * lev), 1) >> 3
    chan = lax.broadcasted_iota(jnp.int32, (lev, 8 * lev), 0)
    repeat = jnp.where(copy_of == chan, 1.0, 0.0).astype(jnp.bfloat16)
    flat = lax.dot_general(
        eof_ref[...], repeat, (((0,), (0,)), ((), ())), preferred_element_type=jnp.float32
    ).astype(jnp.bfloat16)
    row = lax.broadcasted_iota(jnp.int32, (8 * levels, levels), 0) >> 3
    level = lax.broadcasted_iota(jnp.int32, (8 * levels, levels), 1)
    down_all = jnp.where(row == level, 1.0, 0.0).astype(jnp.bfloat16)
    tall = jnp.dot(down_all, flat, preferred_element_type=jnp.float32)
    y_out = lax.broadcasted_iota(jnp.int32, (8 * levels, 8 * lev), 0) & 7
    y_in = lax.broadcasted_iota(jnp.int32, (8 * levels, 8 * lev), 1) & 7
    wide_ref[...] = jnp.where(y_out == y_in, tall, 0.0).astype(jnp.bfloat16)
    stores = [pltpu.make_async_copy(wide_ref, wide_hbm, store.at[GROUPS])]
    stores[0].start()

    def lat_one(c, carry):
        own = lon[c]
        column = jnp.concatenate(
            [
                jnp.concatenate([north[c], own[: 2 * HALO]], axis=0),
                jnp.concatenate([own[TY - 2 * HALO :], south[c]], axis=0),
            ],
            axis=1,
        )
        got = jnp.dot(
            band[c, HALO : 2 * HALO, : 3 * HALO], column, preferred_element_type=jnp.float32
        ).astype(jnp.bfloat16)
        out_ref[c, :HALO] = got[:, :TX]
        out_ref[c, TY - HALO :] = got[:, TX:]
        return carry

    for g in range(GROUPS):

        @pl.when(has_up)
        def _(g=g):
            downs[g].wait_recv()

        @pl.when(has_down)
        def _(g=g):
            ups[g].wait_recv()

        lax.fori_loop(g * width, (g + 1) * width, lat_one, 0, unroll=4)
        chans = pl.ds(g * width, width)
        stores.append(pltpu.make_async_copy(out_ref.at[chans], out_hbm.at[chans], store.at[g]))
        stores[-1].start()

    for copy in stores:
        copy.wait()
    for copy in key_copies + over + [beside] + onward:
        copy.wait_send()
    for g in range(GROUPS):

        @pl.when(has_up)
        def _(g=g):
            ups[g].wait_send()

        @pl.when(has_down)
        def _(g=g):
            downs[g].wait_send()


def mix_kernel(wide_ref, field_ref, out_ref):
    levels = out_ref.shape[0]
    lev = field_ref.shape[0]
    field = field_ref[...].astype(jnp.float32)
    right = jnp.concatenate(
        [field[:, y : y + 8].reshape(8 * lev, TX) for y in range(0, 32, 8)], axis=1
    ).astype(jnp.bfloat16)
    got = jnp.dot(wide_ref[...], right, preferred_element_type=jnp.float32)
    out_ref[...] = jnp.concatenate(
        [got[:, x : x + TX].reshape(levels, 8, TX) for x in range(0, 4 * TX, TX)], axis=1
    ).astype(jnp.bfloat16)


def gathered(innovation, owner_tile, cell_index, length_scale, eof_basis):
    n_lat = lax.axis_size("lat")
    lev, rec = innovation.shape
    levels = eof_basis.shape[0]
    hbm = pl.BlockSpec(memory_space=pltpu.HBM)
    smooth, wide = pl.pallas_call(
        functools.partial(smooth_kernel, n_lat),
        out_shape=(
            jax.ShapeDtypeStruct((lev, TY, TX), jnp.bfloat16),
            jax.ShapeDtypeStruct((8 * levels, 8 * lev), jnp.bfloat16),
        ),
        in_specs=[hbm] * 5,
        out_specs=(hbm, hbm),
        scratch_shapes=[
            pltpu.VMEM((lev, TY, TX), jnp.bfloat16),
            pltpu.VMEM((8 * levels, 8 * lev), jnp.bfloat16),
            pltpu.SemaphoreType.DMA((GROUPS + 1,)),
            pltpu.VMEM((lev, rec), jnp.bfloat16),
            pltpu.VMEM((1, rec), jnp.int32),
            pltpu.VMEM((rec,), jnp.int32),
            pltpu.VMEM((1, lev), jnp.float32),
            pltpu.VMEM((lev, levels), jnp.bfloat16),
            pltpu.SemaphoreType.DMA((5,)),
            pltpu.VMEM((1, rec), jnp.int32),
            pltpu.VMEM((3, lev, rec), jnp.bfloat16),
            pltpu.VMEM((3, 1, rec), jnp.int32),
            pltpu.VMEM((4, 8 * lev, rec), jnp.bfloat16),
            pltpu.VMEM((4, 5, 1, rec), jnp.float32),
            pltpu.VMEM((10, 8 * lev, TX), jnp.float32),
            pltpu.VMEM((lev, TX), jnp.float32),
            pltpu.VMEM((lev, 2 * TX, TX), jnp.bfloat16),
            pltpu.VMEM((lev, TY, TX), jnp.bfloat16),
            pltpu.VMEM((lev, HALO, TX), jnp.bfloat16),
            pltpu.VMEM((lev, HALO, TX), jnp.bfloat16),
            pltpu.SemaphoreType.DMA((5,)),
            pltpu.SemaphoreType.DMA((5,)),
            pltpu.SemaphoreType.DMA((3,)),
            pltpu.SemaphoreType.DMA((3,)),
            pltpu.SemaphoreType.DMA((2, GROUPS)),
            pltpu.SemaphoreType.DMA((2, GROUPS)),
        ],
        compiler_params=pltpu.CompilerParams(
            collective_id=0, has_side_effects=True, vmem_limit_bytes=58 * 1024 * 1024
        ),
        cost_estimate=pl.CostEstimate(
            flops=2 * 8 * lev * 4 * rec * 1280, bytes_accessed=8 * 1024 * 1024, transcendentals=0
        ),
    )(innovation, owner_tile.reshape(1, rec), cell_index, length_scale.reshape(1, lev), eof_basis.T)
    return pl.pallas_call(
        mix_kernel,
        out_shape=jax.ShapeDtypeStruct((levels, TY, TX), jnp.bfloat16),
        grid=(TY // 32,),
        in_specs=[
            pl.BlockSpec((8 * levels, 8 * lev), lambda g: (0, 0)),
            pl.BlockSpec((lev, 32, TX), lambda g: (0, g, 0)),
        ],
        out_specs=pl.BlockSpec((levels, 32, TX), lambda g: (0, g, 0)),
        compiler_params=pltpu.CompilerParams(vmem_limit_bytes=58 * 1024 * 1024),
    )(wide, smooth)


def solution(mesh):
    in_specs = (P(None, ("lon", "lat")), P(("lon", "lat"), None), P(("lon", "lat")), P(), P())
    out_specs = P(None, "lat", "lon")
    local = gathered if mesh.shape["lon"] == 4 else packed
    return jax.shard_map(local, mesh=mesh, in_specs=in_specs, out_specs=out_specs, check_vma=False)
```

```python
import functools

import jax
import jax.numpy as jnp
from jax import lax
from jax.experimental import pallas as pl
from jax.experimental.pallas import tpu as pltpu
from jax.sharding import PartitionSpec as P

TX = 128
TY = 64


def extended(shard, sides, width):
    for axis, dim in sides:
        size, length = (lax.axis_size(axis), shard.shape[dim])
        up = [(i, (i + 1) % size) for i in range(size)]
        down = [(j, i) for i, j in up]
        last = lax.slice_in_dim(shard, length - width, length, axis=dim)
        initial = lax.slice_in_dim(shard, 0, width, axis=dim)
        before = lax.ppermute(last, axis, up)
        after = lax.ppermute(initial, axis, down)
        shard = jnp.concatenate([before, shard, after], axis=dim)
    return shard


def tap_norm(scale):
    dist = jnp.arange(-15, 16).astype(jnp.float32)
    gauss = jnp.exp(-(dist[None, :] * dist[None, :]) / (2.0 * scale[:, None] * scale[:, None]))
    return jnp.sqrt(jnp.sum(gauss * gauss, axis=1))


def tap_weight(dist, scale, norm):
    value = jnp.exp(-(dist * dist) / (2.0 * scale * scale)) / norm
    return jnp.where(jnp.abs(dist) <= 15.0, value, 0.0)


def band_matrix(scale, norm, inner, outer, offset):
    inner_pos = jnp.arange(inner).astype(jnp.float32)[:, None]
    outer_pos = jnp.arange(outer).astype(jnp.float32)[None, :]
    dist = inner_pos - offset - outer_pos
    return tap_weight(dist[None], scale[:, None, None], norm[:, None, None]).astype(jnp.bfloat16)


def slot_numbers(dest, keep, n_lon):
    hits = ((dest[:, None] == jnp.arange(n_lon, dtype=jnp.int32)[None, :]) & keep[:, None]).astype(
        jnp.int32
    )
    before = jnp.cumsum(hits, axis=0) - hits
    return jnp.sum(before * hits, axis=1)


def spread_block(part, where, width):
    cells = jnp.arange(TY * width, dtype=jnp.int32)
    grid_row = (cells // width).astype(jnp.bfloat16)
    grid_col = (cells % width).astype(jnp.bfloat16)
    onehot = (
        (where[0][:, None] == grid_row[None, :]) & (where[1][:, None] == grid_col[None, :])
    ).astype(jnp.bfloat16)
    return jnp.dot(part, onehot, preferred_element_type=jnp.float32)


def packed(innovation, owner_tile, cell_index, length_scale, eof_basis):
    n_lon = lax.axis_size("lon")
    lev, rec = innovation.shape
    cap = (2 * rec + n_lon - 1) // n_lon
    owner = owner_tile[:, 0]
    cell_row = cell_index // TX
    cell_col = cell_index % TX
    everyone = jnp.ones((rec,), jnp.bool_)
    target = owner * cap + slot_numbers(owner, everyone, n_lon)
    values = jnp.zeros((lev, n_lon * cap), jnp.bfloat16).at[:, target].set(innovation)
    coords = jnp.stack([cell_row, cell_col]).astype(jnp.bfloat16)
    places = jnp.full((2, n_lon * cap), -1.0, jnp.bfloat16).at[:, target].set(coords)
    values = values.reshape(lev, n_lon, cap)
    places = places.reshape(2, n_lon, cap)
    got_values, got_places = (
        lax.all_to_all(values, "lon", split_axis=1, concat_axis=1, tiled=True),
        lax.all_to_all(places, "lon", split_axis=1, concat_axis=1, tiled=True),
    )

    def spread_one(source, total):
        part = lax.dynamic_index_in_dim(got_values, source, 1, keepdims=False)
        where = lax.dynamic_index_in_dim(got_places, source, 1, keepdims=False)
        return total + spread_block(part, where, TX)

    summed = lax.fori_loop(0, n_lon, spread_one, jnp.zeros((lev, TY * TX), jnp.float32))
    spread = summed.astype(jnp.bfloat16).reshape(lev, TY, TX)
    padded = extended(spread, (("lon", 2),), 15)
    norm = tap_norm(length_scale)
    band_lon = band_matrix(length_scale, norm, TX + 30, TX, 15.0)
    lon_smooth = jnp.einsum(
        "cyk,ckx->cyx", padded, band_lon, preferred_element_type=jnp.float32
    ).astype(jnp.bfloat16)
    n_lat = lax.axis_size("lat")
    south = [(i, i + 1) for i in range(n_lat - 1)]
    north = [(j, i) for i, j in south]
    above = lax.ppermute(lon_smooth[:, TY - 16 :], "lat", south)
    below = lax.ppermute(lon_smooth[:, :16], "lat", north)
    column = jnp.concatenate([above, lon_smooth, below], axis=1)
    band_lat = band_matrix(length_scale, norm, TY + 32, TY, 16.0)
    smooth = jnp.einsum(
        "cky,ckx->cyx", band_lat, column, preferred_element_type=jnp.float32
    ).astype(jnp.bfloat16)
    return jnp.einsum("lc,cyx->lyx", eof_basis, smooth, preferred_element_type=jnp.float32).astype(
        jnp.bfloat16
    )


MESH = pl.DeviceIdType.MESH
HALO = 16
GROUPS = 4


def copies(ref_from, ref_to, send, recv, target):
    return pltpu.make_async_remote_copy(
        src_ref=ref_from,
        dst_ref=ref_to,
        send_sem=send,
        recv_sem=recv,
        device_id=target,
        device_id_type=MESH,
    )


def smooth_kernel(
    n_lat, innov_hbm, owner_hbm, cell_hbm, scale_hbm, eof_hbm, out_hbm, wide_hbm,
    out_ref, wide_ref, store,
    innov_ref, owner_ref, cell_ref, scale_ref, eof_ref, load, key_ref, vals, keys, picked, codes, sums, weights, band, lon, north, south,
    val_send, val_recv, key_send, key_recv, halo_send, halo_recv,
):
    lev, rec = innov_ref.shape
    levels = eof_ref.shape[1]
    loads = [
        pltpu.make_async_copy(there, here, load.at[i])
        for i, (there, here) in enumerate(
            (
                (owner_hbm, owner_ref),
                (cell_hbm, cell_ref),
                (innov_hbm, innov_ref),
                (scale_hbm, scale_ref),
                (eof_hbm, eof_ref),
            )
        )
    ]
    for copy in loads:
        copy.start()
    half = rec // 2
    me = lax.axis_index("lon")
    lat = lax.axis_index("lat")
    partner = me + 1 - 2 * (me % 2)
    across = (me + 2) % 4
    far = (partner + 2) % 4
    has_up = lat > 0
    has_down = lat < n_lat - 1

    barrier = pltpu.get_barrier_semaphore()
    for peer in (partner, across, far):
        pl.semaphore_signal(barrier, inc=1, device_id=(peer, lat), device_id_type=MESH)

    @pl.when(has_up)
    def _():
        pl.semaphore_signal(barrier, inc=1, device_id=(me, lat - 1), device_id_type=MESH)

    @pl.when(has_down)
    def _():
        pl.semaphore_signal(barrier, inc=1, device_id=(me, lat + 1), device_id_type=MESH)

    loads[0].wait()
    loads[1].wait()
    cell = cell_ref[...].reshape(1, rec)
    key_ref[...] = (cell >> 7) * 512 + owner_ref[...] * TX + (cell & (TX - 1))
    pl.semaphore_wait(barrier, 3 + has_up.astype(jnp.int32) + has_down.astype(jnp.int32))

    key_copies = [
        copies(key_ref, keys.at[i], key_send.at[i], key_recv.at[i], (peer, lat))
        for i, peer in enumerate((partner, across, far))
    ]
    parts = [pl.ds(0, half), pl.ds(half, half)]
    over = [
        copies(
            innov_hbm.at[:, parts[h]], vals.at[1, :, parts[h]],
            val_send.at[h], val_recv.at[h], (across, lat),
        )
        for h in range(2)
    ]
    beside = copies(innov_hbm, vals.at[0], val_send.at[2], val_recv.at[2], (partner, lat))
    onward = [
        copies(
            vals.at[1, :, parts[h]], vals.at[2, :, parts[h]],
            val_send.at[3 + h], val_recv.at[3 + h], (partner, lat),
        )
        for h in range(2)
    ]
    for copy in key_copies:
        copy.start()
    over[0].start()
    over[1].start()
    beside.start()

    column = lax.broadcasted_iota(jnp.int32, (rec, TX), 1).astype(jnp.float32)
    zero = jnp.zeros((), jnp.bfloat16)

    def sort_out(part, key, at):
        row = key >> 9
        rel = ((key & 511) - TX * me + HALO) & 511
        sub = (row & 7).astype(jnp.float32).astype(jnp.bfloat16)
        phase = row >> 3
        inside = (rel >= HALO) & (rel < HALO + TX)
        pair = phase >> 1
        start = jnp.where(pair == 0, 0, jnp.where(pair == 3, 2 * TX, 4 * TX + pair * 2 * TX))
        main = start + (phase & 1) * TX + rel - HALO
        rim_hit = (rel < HALO) | ((rel >= HALO + TX) & (rel < 2 * HALO + TX))
        rim = 4 * TX + phase * 2 * HALO + jnp.where(rel < HALO, rel, rel - TX)
        code = jnp.where(inside, main, jnp.where(rim_hit, rim, -1)).astype(jnp.float32)
        codes[at] = jnp.broadcast_to(code, (TX, rec)).T
        values = part[...]
        for t in range(8):
            mine = sub == jnp.full((), t, jnp.bfloat16)
            picked[at, pl.ds(t * lev, lev), :] = jnp.where(mine, values, zero)

    def spread(blocks, tiles, first=False):
        got = None
        for at in blocks:
            code = codes[at]
            onehot = jnp.concatenate(
                [
                    jnp.where(code == column + float(i * TX), 1.0, 0.0).astype(jnp.bfloat16)
                    for i in range(2 * tiles[0], 2 * tiles[1])
                ],
                axis=1,
            )
            term = jnp.dot(picked[at], onehot, preferred_element_type=jnp.float32)
            got = term if got is None else got + term
        for i in range(2 * (tiles[1] - tiles[0])):
            piece = got[:, i * TX : (i + 1) * TX]
            if first:
                sums[2 * tiles[0] + i] = piece
            else:
                sums[2 * tiles[0] + i] += piece

    loads[2].wait()
    sort_out(innov_ref, key_ref[...], 0)
    spread([0], (0, 3), True)

    line = lax.broadcasted_iota(jnp.int32, (lev, TX), 1)
    near = jnp.where(line < TX // 2, line, line - TX).astype(jnp.float32)
    loads[3].wait()
    diagonal = lax.broadcasted_iota(jnp.int32, (lev, lev), 0) == lax.broadcasted_iota(
        jnp.int32, (lev, lev), 1
    )
    scale = jnp.sum(
        jnp.where(diagonal, jnp.broadcast_to(scale_ref[...], (lev, lev)), 0.0), axis=1, keepdims=True
    )
    gauss = jnp.where(
        jnp.abs(near) <= 15.0, jnp.exp(-(near * near) / (2.0 * scale * scale)), 0.0
    )
    norm = jnp.sqrt(jnp.sum(gauss * gauss, axis=1, keepdims=True))
    weights[...] = gauss / norm
    down_at = lax.broadcasted_iota(jnp.int32, (TX, TX), 0)
    side_at = lax.broadcasted_iota(jnp.int32, (TX, TX), 1)
    straight = jnp.abs(down_at - side_at) < TX // 2
    west = side_at[:HALO] < TX // 2

    def band_one(c, carry):
        ring = pltpu.roll(
            jnp.broadcast_to(weights[pl.ds(c, 1), :], (TX, TX)), 0, 1, stride=1, stride_axis=0
        )
        band[c, :TX] = jnp.where(straight, ring, 0.0).astype(jnp.bfloat16)
        rim = jnp.concatenate(
            [jnp.where(west, ring[TX - HALO :], 0.0), jnp.where(west, 0.0, ring[:HALO])], axis=0
        ).astype(jnp.bfloat16)
        for t in range(4):
            band[c, TX + 2 * HALO * t : TX + 2 * HALO * (t + 1)] = rim
        return carry

    lax.fori_loop(0, lev, band_one, 0, unroll=4)

    key_copies[0].wait_recv()
    beside.wait_recv()
    sort_out(vals.at[0], keys[0], 1)
    spread([1], (0, 3))
    for h in range(2):
        over[h].wait_recv()
        onward[h].start()
    key_copies[1].wait_recv()
    sort_out(vals.at[1], keys[1], 2)
    spread([2], (0, 3))
    key_copies[2].wait_recv()
    for h in range(2):
        onward[h].wait_recv()
    sort_out(vals.at[2], keys[2], 3)
    spread([3], (0, 3))

    lane = lax.broadcasted_iota(jnp.int32, (8, TX), 1) >> 5
    width = lev // GROUPS
    spot = (0, 1, 6, 7, 8, 9, 2, 3)

    def lon_rows(c, phases):
        rows = pl.ds(c, 8, stride=lev)
        main = [sums[spot[p], rows, :] for p in phases]
        rim = [jnp.where(lane == p % 4, sums[4 + p // 4, rows, :], 0.0) for p in phases]
        left = jnp.concatenate(
            [jnp.concatenate(main, axis=0), jnp.concatenate(rim, axis=0)], axis=1
        ).astype(jnp.bfloat16)
        return jnp.dot(left, band[c], preferred_element_type=jnp.float32).astype(jnp.bfloat16)

    def lon_one(c, carry):
        got = lon_rows(c, (0, 1, 6, 7))
        lon[c, :HALO] = got[:HALO]
        lon[c, TY - HALO :] = got[HALO:]
        return carry

    def mid_one(c, carry):
        lon[c, HALO : TY - HALO] = lon_rows(c, (2, 3, 4, 5))
        return carry

    def inner_one(c, carry):
        out_ref[c, HALO : TY - HALO] = jnp.dot(
            band[c, HALO : TY - HALO, :TY], lon[c], preferred_element_type=jnp.float32
        ).astype(jnp.bfloat16)
        return carry

    ups, downs = [], []
    for g in range(GROUPS):
        lax.fori_loop(g * width, (g + 1) * width, lon_one, 0, unroll=8)
        chans = pl.ds(g * width, width)
        up = copies(
            lon.at[chans, pl.ds(0, HALO), :], south.at[chans],
            halo_send.at[0, g], halo_recv.at[0, g], (me, lat - 1),
        )
        down = copies(
            lon.at[chans, pl.ds(TY - HALO, HALO), :], north.at[chans],
            halo_send.at[1, g], halo_recv.at[1, g], (me, lat + 1),
        )
        ups.append(up)
        downs.append(down)

        @pl.when(has_up)
        def _(up=up):
            up.start()

        @pl.when(has_down)
        def _(down=down):
            down.start()

    @pl.when(jnp.logical_not(has_up))
    def _():
        north[...] = jnp.zeros_like(north)

    @pl.when(jnp.logical_not(has_down))
    def _():
        south[...] = jnp.zeros_like(south)

    spread([0, 1, 2, 3], (3, 5), True)
    lax.fori_loop(0, lev, mid_one, 0, unroll=8)
    lax.fori_loop(0, lev, inner_one, 0, unroll=8)

    loads[4].wait()
    copy_of = lax.broadcasted_iota(jnp.int32, (lev, 8 * lev), 1) >> 3
    chan = lax.broadcasted_iota(jnp.int32, (lev, 8 * lev), 0)
    repeat = jnp.where(copy_of == chan, 1.0, 0.0).astype(jnp.bfloat16)
    flat = lax.dot_general(
        eof_ref[...], repeat, (((0,), (0,)), ((), ())), preferred_element_type=jnp.float32
    ).astype(jnp.bfloat16)
    row = lax.broadcasted_iota(jnp.int32, (8 * levels, levels), 0) >> 3
    level = lax.broadcasted_iota(jnp.int32, (8 * levels, levels), 1)
    down_all = jnp.where(row == level, 1.0, 0.0).astype(jnp.bfloat16)
    tall = jnp.dot(down_all, flat, preferred_element_type=jnp.float32)
    y_out = lax.broadcasted_iota(jnp.int32, (8 * levels, 8 * lev), 0) & 7
    y_in = lax.broadcasted_iota(jnp.int32, (8 * levels, 8 * lev), 1) & 7
    wide_ref[...] = jnp.where(y_out == y_in, tall, 0.0).astype(jnp.bfloat16)
    stores = [pltpu.make_async_copy(wide_ref, wide_hbm, store.at[GROUPS])]
    stores[0].start()

    def lat_one(c, carry):
        own = lon[c]
        column = jnp.concatenate(
            [
                jnp.concatenate([north[c], own[: 2 * HALO]], axis=0),
                jnp.concatenate([own[TY - 2 * HALO :], south[c]], axis=0),
            ],
            axis=1,
        )
        got = jnp.dot(
            band[c, HALO : 2 * HALO, : 3 * HALO], column, preferred_element_type=jnp.float32
        ).astype(jnp.bfloat16)
        out_ref[c, :HALO] = got[:, :TX]
        out_ref[c, TY - HALO :] = got[:, TX:]
        return carry

    for g in range(GROUPS):

        @pl.when(has_up)
        def _(g=g):
            downs[g].wait_recv()

        @pl.when(has_down)
        def _(g=g):
            ups[g].wait_recv()

        lax.fori_loop(g * width, (g + 1) * width, lat_one, 0, unroll=8)
        chans = pl.ds(g * width, width)
        stores.append(pltpu.make_async_copy(out_ref.at[chans], out_hbm.at[chans], store.at[g]))
        stores[-1].start()

    for copy in stores:
        copy.wait()
    for copy in key_copies + over + [beside] + onward:
        copy.wait_send()
    for g in range(GROUPS):

        @pl.when(has_up)
        def _(g=g):
            ups[g].wait_send()

        @pl.when(has_down)
        def _(g=g):
            downs[g].wait_send()


def mix_kernel(wide_ref, field_ref, out_ref):
    levels = out_ref.shape[0]
    lev = field_ref.shape[0]
    field = field_ref[...].astype(jnp.float32)
    right = jnp.concatenate(
        [field[:, y : y + 8].reshape(8 * lev, TX) for y in range(0, 32, 8)], axis=1
    ).astype(jnp.bfloat16)
    got = jnp.dot(wide_ref[...], right, preferred_element_type=jnp.float32)
    out_ref[...] = jnp.concatenate(
        [got[:, x : x + TX].reshape(levels, 8, TX) for x in range(0, 4 * TX, TX)], axis=1
    ).astype(jnp.bfloat16)


def gathered(innovation, owner_tile, cell_index, length_scale, eof_basis):
    n_lat = lax.axis_size("lat")
    lev, rec = innovation.shape
    levels = eof_basis.shape[0]
    hbm = pl.BlockSpec(memory_space=pltpu.HBM)
    smooth, wide = pl.pallas_call(
        functools.partial(smooth_kernel, n_lat),
        out_shape=(
            jax.ShapeDtypeStruct((lev, TY, TX), jnp.bfloat16),
            jax.ShapeDtypeStruct((8 * levels, 8 * lev), jnp.bfloat16),
        ),
        in_specs=[hbm] * 5,
        out_specs=(hbm, hbm),
        scratch_shapes=[
            pltpu.VMEM((lev, TY, TX), jnp.bfloat16),
            pltpu.VMEM((8 * levels, 8 * lev), jnp.bfloat16),
            pltpu.SemaphoreType.DMA((GROUPS + 1,)),
            pltpu.VMEM((lev, rec), jnp.bfloat16),
            pltpu.VMEM((1, rec), jnp.int32),
            pltpu.VMEM((rec,), jnp.int32),
            pltpu.VMEM((1, lev), jnp.float32),
            pltpu.VMEM((lev, levels), jnp.bfloat16),
            pltpu.SemaphoreType.DMA((5,)),
            pltpu.VMEM((1, rec), jnp.int32),
            pltpu.VMEM((3, lev, rec), jnp.bfloat16),
            pltpu.VMEM((3, 1, rec), jnp.int32),
            pltpu.VMEM((4, 8 * lev, rec), jnp.bfloat16),
            pltpu.VMEM((4, rec, TX), jnp.float32),
            pltpu.VMEM((10, 8 * lev, TX), jnp.float32),
            pltpu.VMEM((lev, TX), jnp.float32),
            pltpu.VMEM((lev, 2 * TX, TX), jnp.bfloat16),
            pltpu.VMEM((lev, TY, TX), jnp.bfloat16),
            pltpu.VMEM((lev, HALO, TX), jnp.bfloat16),
            pltpu.VMEM((lev, HALO, TX), jnp.bfloat16),
            pltpu.SemaphoreType.DMA((5,)),
            pltpu.SemaphoreType.DMA((5,)),
            pltpu.SemaphoreType.DMA((3,)),
            pltpu.SemaphoreType.DMA((3,)),
            pltpu.SemaphoreType.DMA((2, GROUPS)),
            pltpu.SemaphoreType.DMA((2, GROUPS)),
        ],
        compiler_params=pltpu.CompilerParams(
            collective_id=0, has_side_effects=True, vmem_limit_bytes=58 * 1024 * 1024
        ),
        cost_estimate=pl.CostEstimate(
            flops=2 * 8 * lev * 4 * rec * 1280, bytes_accessed=8 * 1024 * 1024, transcendentals=0
        ),
    )(innovation, owner_tile.reshape(1, rec), cell_index, length_scale.reshape(1, lev), eof_basis.T)
    return pl.pallas_call(
        mix_kernel,
        out_shape=jax.ShapeDtypeStruct((levels, TY, TX), jnp.bfloat16),
        grid=(TY // 32,),
        in_specs=[
            pl.BlockSpec((8 * levels, 8 * lev), lambda g: (0, 0)),
            pl.BlockSpec((lev, 32, TX), lambda g: (0, g, 0)),
        ],
        out_specs=pl.BlockSpec((levels, 32, TX), lambda g: (0, g, 0)),
        compiler_params=pltpu.CompilerParams(vmem_limit_bytes=58 * 1024 * 1024),
    )(wide, smooth)


def solution(mesh):
    in_specs = (P(None, ("lon", "lat")), P(("lon", "lat"), None), P(("lon", "lat")), P(), P())
    out_specs = P(None, "lat", "lon")
    local = gathered if mesh.shape["lon"] == 4 else packed
    return jax.shard_map(local, mesh=mesh, in_specs=in_specs, out_specs=out_specs, check_vma=False)
```

```python
import functools

import jax
import jax.numpy as jnp
from jax import lax
from jax.experimental import pallas as pl
from jax.experimental.pallas import tpu as pltpu
from jax.sharding import PartitionSpec as P

TX = 128
TY = 64


def extended(shard, sides, width):
    for axis, dim in sides:
        size, length = (lax.axis_size(axis), shard.shape[dim])
        up = [(i, (i + 1) % size) for i in range(size)]
        down = [(j, i) for i, j in up]
        last = lax.slice_in_dim(shard, length - width, length, axis=dim)
        initial = lax.slice_in_dim(shard, 0, width, axis=dim)
        before = lax.ppermute(last, axis, up)
        after = lax.ppermute(initial, axis, down)
        shard = jnp.concatenate([before, shard, after], axis=dim)
    return shard


def tap_norm(scale):
    dist = jnp.arange(-15, 16).astype(jnp.float32)
    gauss = jnp.exp(-(dist[None, :] * dist[None, :]) / (2.0 * scale[:, None] * scale[:, None]))
    return jnp.sqrt(jnp.sum(gauss * gauss, axis=1))


def tap_weight(dist, scale, norm):
    value = jnp.exp(-(dist * dist) / (2.0 * scale * scale)) / norm
    return jnp.where(jnp.abs(dist) <= 15.0, value, 0.0)


def band_matrix(scale, norm, inner, outer, offset):
    inner_pos = jnp.arange(inner).astype(jnp.float32)[:, None]
    outer_pos = jnp.arange(outer).astype(jnp.float32)[None, :]
    dist = inner_pos - offset - outer_pos
    return tap_weight(dist[None], scale[:, None, None], norm[:, None, None]).astype(jnp.bfloat16)


def slot_numbers(dest, keep, n_lon):
    hits = ((dest[:, None] == jnp.arange(n_lon, dtype=jnp.int32)[None, :]) & keep[:, None]).astype(
        jnp.int32
    )
    before = jnp.cumsum(hits, axis=0) - hits
    return jnp.sum(before * hits, axis=1)


def spread_block(part, where, width):
    cells = jnp.arange(TY * width, dtype=jnp.int32)
    grid_row = (cells // width).astype(jnp.bfloat16)
    grid_col = (cells % width).astype(jnp.bfloat16)
    onehot = (
        (where[0][:, None] == grid_row[None, :]) & (where[1][:, None] == grid_col[None, :])
    ).astype(jnp.bfloat16)
    return jnp.dot(part, onehot, preferred_element_type=jnp.float32)


def packed(innovation, owner_tile, cell_index, length_scale, eof_basis):
    n_lon = lax.axis_size("lon")
    lev, rec = innovation.shape
    cap = (2 * rec + n_lon - 1) // n_lon
    owner = owner_tile[:, 0]
    cell_row = cell_index // TX
    cell_col = cell_index % TX
    everyone = jnp.ones((rec,), jnp.bool_)
    target = owner * cap + slot_numbers(owner, everyone, n_lon)
    values = jnp.zeros((lev, n_lon * cap), jnp.bfloat16).at[:, target].set(innovation)
    coords = jnp.stack([cell_row, cell_col]).astype(jnp.bfloat16)
    places = jnp.full((2, n_lon * cap), -1.0, jnp.bfloat16).at[:, target].set(coords)
    values = values.reshape(lev, n_lon, cap)
    places = places.reshape(2, n_lon, cap)
    got_values, got_places = (
        lax.all_to_all(values, "lon", split_axis=1, concat_axis=1, tiled=True),
        lax.all_to_all(places, "lon", split_axis=1, concat_axis=1, tiled=True),
    )

    def spread_one(source, total):
        part = lax.dynamic_index_in_dim(got_values, source, 1, keepdims=False)
        where = lax.dynamic_index_in_dim(got_places, source, 1, keepdims=False)
        return total + spread_block(part, where, TX)

    summed = lax.fori_loop(0, n_lon, spread_one, jnp.zeros((lev, TY * TX), jnp.float32))
    spread = summed.astype(jnp.bfloat16).reshape(lev, TY, TX)
    padded = extended(spread, (("lon", 2),), 15)
    norm = tap_norm(length_scale)
    band_lon = band_matrix(length_scale, norm, TX + 30, TX, 15.0)
    lon_smooth = jnp.einsum(
        "cyk,ckx->cyx", padded, band_lon, preferred_element_type=jnp.float32
    ).astype(jnp.bfloat16)
    n_lat = lax.axis_size("lat")
    south = [(i, i + 1) for i in range(n_lat - 1)]
    north = [(j, i) for i, j in south]
    above = lax.ppermute(lon_smooth[:, TY - 16 :], "lat", south)
    below = lax.ppermute(lon_smooth[:, :16], "lat", north)
    column = jnp.concatenate([above, lon_smooth, below], axis=1)
    band_lat = band_matrix(length_scale, norm, TY + 32, TY, 16.0)
    smooth = jnp.einsum(
        "cky,ckx->cyx", band_lat, column, preferred_element_type=jnp.float32
    ).astype(jnp.bfloat16)
    return jnp.einsum("lc,cyx->lyx", eof_basis, smooth, preferred_element_type=jnp.float32).astype(
        jnp.bfloat16
    )


MESH = pl.DeviceIdType.MESH
HALO = 16
GROUPS = 8


def copies(ref_from, ref_to, send, recv, target):
    return pltpu.make_async_remote_copy(
        src_ref=ref_from,
        dst_ref=ref_to,
        send_sem=send,
        recv_sem=recv,
        device_id=target,
        device_id_type=MESH,
    )


def smooth_kernel(
    n_lat, innov_hbm, owner_hbm, cell_hbm, scale_hbm, eof_hbm, out_hbm, wide_hbm,
    out_ref, wide_ref, store,
    innov_ref, owner_ref, cell_ref, scale_ref, eof_ref, load, key_ref, vals, keys, picked, codes, sums, weights, band, lon, north, south,
    val_send, val_recv, key_send, key_recv, halo_send, halo_recv,
):
    lev, rec = innov_ref.shape
    levels = eof_ref.shape[1]
    loads = [
        pltpu.make_async_copy(there, here, load.at[i])
        for i, (there, here) in enumerate(
            (
                (owner_hbm, owner_ref),
                (cell_hbm, cell_ref),
                (innov_hbm, innov_ref),
                (scale_hbm, scale_ref),
                (eof_hbm, eof_ref),
            )
        )
    ]
    for copy in loads:
        copy.start()
    half = rec // 2
    me = lax.axis_index("lon")
    lat = lax.axis_index("lat")
    partner = me + 1 - 2 * (me % 2)
    across = (me + 2) % 4
    far = (partner + 2) % 4
    has_up = lat > 0
    has_down = lat < n_lat - 1

    barrier = pltpu.get_barrier_semaphore()
    for peer in (partner, across, far):
        pl.semaphore_signal(barrier, inc=1, device_id=(peer, lat), device_id_type=MESH)

    @pl.when(has_up)
    def _():
        pl.semaphore_signal(barrier, inc=1, device_id=(me, lat - 1), device_id_type=MESH)

    @pl.when(has_down)
    def _():
        pl.semaphore_signal(barrier, inc=1, device_id=(me, lat + 1), device_id_type=MESH)

    loads[0].wait()
    loads[1].wait()
    cell = cell_ref[...].reshape(1, rec)
    key_ref[...] = (cell >> 7) * 512 + owner_ref[...] * TX + (cell & (TX - 1))
    pl.semaphore_wait(barrier, 3 + has_up.astype(jnp.int32) + has_down.astype(jnp.int32))

    key_copies = [
        copies(key_ref, keys.at[i], key_send.at[i], key_recv.at[i], (peer, lat))
        for i, peer in enumerate((partner, across, far))
    ]
    parts = [pl.ds(0, half), pl.ds(half, half)]
    over = [
        copies(
            innov_hbm.at[:, parts[h]], vals.at[1, :, parts[h]],
            val_send.at[h], val_recv.at[h], (across, lat),
        )
        for h in range(2)
    ]
    beside = copies(innov_hbm, vals.at[0], val_send.at[2], val_recv.at[2], (partner, lat))
    onward = [
        copies(
            vals.at[1, :, parts[h]], vals.at[2, :, parts[h]],
            val_send.at[3 + h], val_recv.at[3 + h], (partner, lat),
        )
        for h in range(2)
    ]
    for copy in key_copies:
        copy.start()
    over[0].start()
    over[1].start()
    beside.start()

    column = lax.broadcasted_iota(jnp.int32, (rec, TX), 1).astype(jnp.float32)
    zero = jnp.zeros((), jnp.bfloat16)

    def sort_out(part, key, at):
        row = key >> 9
        rel = ((key & 511) - TX * me + HALO) & 511
        sub = (row & 7).astype(jnp.float32).astype(jnp.bfloat16)
        phase = row >> 3
        inside = (rel >= HALO) & (rel < HALO + TX)
        pair = phase >> 1
        start = jnp.where(pair == 0, 0, jnp.where(pair == 3, 2 * TX, 4 * TX + pair * 2 * TX))
        main = start + (phase & 1) * TX + rel - HALO
        rim_hit = (rel < HALO) | ((rel >= HALO + TX) & (rel < 2 * HALO + TX))
        rim = 4 * TX + phase * 2 * HALO + jnp.where(rel < HALO, rel, rel - TX)
        code = jnp.where(inside, main, jnp.where(rim_hit, rim, -1)).astype(jnp.float32)
        codes[at] = jnp.broadcast_to(code, (TX, rec)).T
        values = part[...]
        for t in range(8):
            mine = sub == jnp.full((), t, jnp.bfloat16)
            picked[at, pl.ds(t * lev, lev), :] = jnp.where(mine, values, zero)

    def spread(blocks, tiles, first=False):
        got = None
        for at in blocks:
            code = codes[at]
            onehot = jnp.concatenate(
                [
                    jnp.where(code == column + float(i * TX), 1.0, 0.0).astype(jnp.bfloat16)
                    for i in range(2 * tiles[0], 2 * tiles[1])
                ],
                axis=1,
            )
            term = jnp.dot(picked[at], onehot, preferred_element_type=jnp.float32)
            got = term if got is None else got + term
        for i in range(2 * (tiles[1] - tiles[0])):
            piece = got[:, i * TX : (i + 1) * TX]
            if first:
                sums[2 * tiles[0] + i] = piece
            else:
                sums[2 * tiles[0] + i] += piece

    loads[2].wait()
    sort_out(innov_ref, key_ref[...], 0)
    spread([0], (0, 3), True)

    line = lax.broadcasted_iota(jnp.int32, (lev, TX), 1)
    near = jnp.where(line < TX // 2, line, line - TX).astype(jnp.float32)
    loads[3].wait()
    diagonal = lax.broadcasted_iota(jnp.int32, (lev, lev), 0) == lax.broadcasted_iota(
        jnp.int32, (lev, lev), 1
    )
    scale = jnp.sum(
        jnp.where(diagonal, jnp.broadcast_to(scale_ref[...], (lev, lev)), 0.0), axis=1, keepdims=True
    )
    gauss = jnp.where(
        jnp.abs(near) <= 15.0, jnp.exp(-(near * near) / (2.0 * scale * scale)), 0.0
    )
    norm = jnp.sqrt(jnp.sum(gauss * gauss, axis=1, keepdims=True))
    weights[...] = gauss / norm
    down_at = lax.broadcasted_iota(jnp.int32, (TX, TX), 0)
    side_at = lax.broadcasted_iota(jnp.int32, (TX, TX), 1)
    straight = jnp.abs(down_at - side_at) < TX // 2
    west = side_at[:HALO] < TX // 2

    def band_one(c, carry):
        ring = pltpu.roll(
            jnp.broadcast_to(weights[pl.ds(c, 1), :], (TX, TX)), 0, 1, stride=1, stride_axis=0
        )
        band[c, :TX] = jnp.where(straight, ring, 0.0).astype(jnp.bfloat16)
        rim = jnp.concatenate(
            [jnp.where(west, ring[TX - HALO :], 0.0), jnp.where(west, 0.0, ring[:HALO])], axis=0
        ).astype(jnp.bfloat16)
        for t in range(4):
            band[c, TX + 2 * HALO * t : TX + 2 * HALO * (t + 1)] = rim
        return carry

    lax.fori_loop(0, lev, band_one, 0, unroll=4)

    key_copies[0].wait_recv()
    beside.wait_recv()
    sort_out(vals.at[0], keys[0], 1)
    spread([1], (0, 3))
    for h in range(2):
        over[h].wait_recv()
        onward[h].start()
    key_copies[1].wait_recv()
    sort_out(vals.at[1], keys[1], 2)
    spread([2], (0, 3))
    key_copies[2].wait_recv()
    for h in range(2):
        onward[h].wait_recv()
    sort_out(vals.at[2], keys[2], 3)
    spread([3], (0, 3))

    lane = lax.broadcasted_iota(jnp.int32, (8, TX), 1) >> 5
    width = lev // GROUPS
    spot = (0, 1, 6, 7, 8, 9, 2, 3)

    def lon_rows(c, phases):
        rows = pl.ds(c, 8, stride=lev)
        main = [sums[spot[p], rows, :] for p in phases]
        rim = [jnp.where(lane == p % 4, sums[4 + p // 4, rows, :], 0.0) for p in phases]
        left = jnp.concatenate(
            [jnp.concatenate(main, axis=0), jnp.concatenate(rim, axis=0)], axis=1
        ).astype(jnp.bfloat16)
        return jnp.dot(left, band[c], preferred_element_type=jnp.float32).astype(jnp.bfloat16)

    def lon_one(c, carry):
        got = lon_rows(c, (0, 1, 6, 7))
        lon[c, :HALO] = got[:HALO]
        lon[c, TY - HALO :] = got[HALO:]
        return carry

    def mid_one(c, carry):
        lon[c, HALO : TY - HALO] = lon_rows(c, (2, 3, 4, 5))
        return carry

    def inner_one(c, carry):
        out_ref[c, HALO : TY - HALO] = jnp.dot(
            band[c, HALO : TY - HALO, :TY], lon[c], preferred_element_type=jnp.float32
        ).astype(jnp.bfloat16)
        return carry

    ups, downs = [], []
    for g in range(GROUPS):
        lax.fori_loop(g * width, (g + 1) * width, lon_one, 0, unroll=8)
        chans = pl.ds(g * width, width)
        up = copies(
            lon.at[chans, pl.ds(0, HALO), :], south.at[chans],
            halo_send.at[0, g], halo_recv.at[0, g], (me, lat - 1),
        )
        down = copies(
            lon.at[chans, pl.ds(TY - HALO, HALO), :], north.at[chans],
            halo_send.at[1, g], halo_recv.at[1, g], (me, lat + 1),
        )
        ups.append(up)
        downs.append(down)

        @pl.when(has_up)
        def _(up=up):
            up.start()

        @pl.when(has_down)
        def _(down=down):
            down.start()

    @pl.when(jnp.logical_not(has_up))
    def _():
        north[...] = jnp.zeros_like(north)

    @pl.when(jnp.logical_not(has_down))
    def _():
        south[...] = jnp.zeros_like(south)

    spread([0, 1, 2, 3], (3, 5), True)
    lax.fori_loop(0, lev, mid_one, 0, unroll=8)
    lax.fori_loop(0, lev, inner_one, 0, unroll=8)

    loads[4].wait()
    copy_of = lax.broadcasted_iota(jnp.int32, (lev, 8 * lev), 1) >> 3
    chan = lax.broadcasted_iota(jnp.int32, (lev, 8 * lev), 0)
    repeat = jnp.where(copy_of == chan, 1.0, 0.0).astype(jnp.bfloat16)
    flat = lax.dot_general(
        eof_ref[...], repeat, (((0,), (0,)), ((), ())), preferred_element_type=jnp.float32
    ).astype(jnp.bfloat16)
    row = lax.broadcasted_iota(jnp.int32, (8 * levels, levels), 0) >> 3
    level = lax.broadcasted_iota(jnp.int32, (8 * levels, levels), 1)
    down_all = jnp.where(row == level, 1.0, 0.0).astype(jnp.bfloat16)
    tall = jnp.dot(down_all, flat, preferred_element_type=jnp.float32)
    y_out = lax.broadcasted_iota(jnp.int32, (8 * levels, 8 * lev), 0) & 7
    y_in = lax.broadcasted_iota(jnp.int32, (8 * levels, 8 * lev), 1) & 7
    wide_ref[...] = jnp.where(y_out == y_in, tall, 0.0).astype(jnp.bfloat16)
    stores = [pltpu.make_async_copy(wide_ref, wide_hbm, store.at[GROUPS])]
    stores[0].start()

    def lat_one(c, carry):
        own = lon[c]
        column = jnp.concatenate(
            [
                jnp.concatenate([north[c], own[: 2 * HALO]], axis=0),
                jnp.concatenate([own[TY - 2 * HALO :], south[c]], axis=0),
            ],
            axis=1,
        )
        got = jnp.dot(
            band[c, HALO : 2 * HALO, : 3 * HALO], column, preferred_element_type=jnp.float32
        ).astype(jnp.bfloat16)
        out_ref[c, :HALO] = got[:, :TX]
        out_ref[c, TY - HALO :] = got[:, TX:]
        return carry

    for g in range(GROUPS):

        @pl.when(has_up)
        def _(g=g):
            downs[g].wait_recv()

        @pl.when(has_down)
        def _(g=g):
            ups[g].wait_recv()

        lax.fori_loop(g * width, (g + 1) * width, lat_one, 0, unroll=8)
        chans = pl.ds(g * width, width)
        stores.append(pltpu.make_async_copy(out_ref.at[chans], out_hbm.at[chans], store.at[g]))
        stores[-1].start()

    for copy in stores:
        copy.wait()
    for copy in key_copies + over + [beside] + onward:
        copy.wait_send()
    for g in range(GROUPS):

        @pl.when(has_up)
        def _(g=g):
            ups[g].wait_send()

        @pl.when(has_down)
        def _(g=g):
            downs[g].wait_send()


def mix_kernel(wide_ref, field_ref, out_ref):
    levels = out_ref.shape[0]
    lev = field_ref.shape[0]
    field = field_ref[...].astype(jnp.float32)
    right = jnp.concatenate(
        [field[:, y : y + 8].reshape(8 * lev, TX) for y in range(0, 32, 8)], axis=1
    ).astype(jnp.bfloat16)
    got = jnp.dot(wide_ref[...], right, preferred_element_type=jnp.float32)
    out_ref[...] = jnp.concatenate(
        [got[:, x : x + TX].reshape(levels, 8, TX) for x in range(0, 4 * TX, TX)], axis=1
    ).astype(jnp.bfloat16)


def gathered(innovation, owner_tile, cell_index, length_scale, eof_basis):
    n_lat = lax.axis_size("lat")
    lev, rec = innovation.shape
    levels = eof_basis.shape[0]
    hbm = pl.BlockSpec(memory_space=pltpu.HBM)
    smooth, wide = pl.pallas_call(
        functools.partial(smooth_kernel, n_lat),
        out_shape=(
            jax.ShapeDtypeStruct((lev, TY, TX), jnp.bfloat16),
            jax.ShapeDtypeStruct((8 * levels, 8 * lev), jnp.bfloat16),
        ),
        in_specs=[hbm] * 5,
        out_specs=(hbm, hbm),
        scratch_shapes=[
            pltpu.VMEM((lev, TY, TX), jnp.bfloat16),
            pltpu.VMEM((8 * levels, 8 * lev), jnp.bfloat16),
            pltpu.SemaphoreType.DMA((GROUPS + 1,)),
            pltpu.VMEM((lev, rec), jnp.bfloat16),
            pltpu.VMEM((1, rec), jnp.int32),
            pltpu.VMEM((rec,), jnp.int32),
            pltpu.VMEM((1, lev), jnp.float32),
            pltpu.VMEM((lev, levels), jnp.bfloat16),
            pltpu.SemaphoreType.DMA((5,)),
            pltpu.VMEM((1, rec), jnp.int32),
            pltpu.VMEM((3, lev, rec), jnp.bfloat16),
            pltpu.VMEM((3, 1, rec), jnp.int32),
            pltpu.VMEM((4, 8 * lev, rec), jnp.bfloat16),
            pltpu.VMEM((4, rec, TX), jnp.float32),
            pltpu.VMEM((10, 8 * lev, TX), jnp.float32),
            pltpu.VMEM((lev, TX), jnp.float32),
            pltpu.VMEM((lev, 2 * TX, TX), jnp.bfloat16),
            pltpu.VMEM((lev, TY, TX), jnp.bfloat16),
            pltpu.VMEM((lev, HALO, TX), jnp.bfloat16),
            pltpu.VMEM((lev, HALO, TX), jnp.bfloat16),
            pltpu.SemaphoreType.DMA((5,)),
            pltpu.SemaphoreType.DMA((5,)),
            pltpu.SemaphoreType.DMA((3,)),
            pltpu.SemaphoreType.DMA((3,)),
            pltpu.SemaphoreType.DMA((2, GROUPS)),
            pltpu.SemaphoreType.DMA((2, GROUPS)),
        ],
        compiler_params=pltpu.CompilerParams(
            collective_id=0, has_side_effects=True, vmem_limit_bytes=58 * 1024 * 1024
        ),
        cost_estimate=pl.CostEstimate(
            flops=2 * 8 * lev * 4 * rec * 1280, bytes_accessed=8 * 1024 * 1024, transcendentals=0
        ),
    )(innovation, owner_tile.reshape(1, rec), cell_index, length_scale.reshape(1, lev), eof_basis.T)
    return pl.pallas_call(
        mix_kernel,
        out_shape=jax.ShapeDtypeStruct((levels, TY, TX), jnp.bfloat16),
        grid=(TY // 32,),
        in_specs=[
            pl.BlockSpec((8 * levels, 8 * lev), lambda g: (0, 0)),
            pl.BlockSpec((lev, 32, TX), lambda g: (0, g, 0)),
        ],
        out_specs=pl.BlockSpec((levels, 32, TX), lambda g: (0, g, 0)),
        compiler_params=pltpu.CompilerParams(vmem_limit_bytes=58 * 1024 * 1024),
    )(wide, smooth)


def solution(mesh):
    in_specs = (P(None, ("lon", "lat")), P(("lon", "lat"), None), P(("lon", "lat")), P(), P())
    out_specs = P(None, "lat", "lon")
    local = gathered if mesh.shape["lon"] == 4 else packed
    return jax.shard_map(local, mesh=mesh, in_specs=in_specs, out_specs=out_specs, check_vma=False)
```
